32 devices in a mesh: seq: 8 (over z, y), head: 4 (over x, core).
Axes of the slice: x: 2, y: 2, z: 4, core: 2. Of those that a mesh axis runs over, the one named last changes fastest.
Arguments:
- features: bfloat16 [20480, 8192], P('seq', 'head'), may hold values from -75 to 75
- state_write: bfloat16 [20480, 128], P('seq'), may hold values from -6 to 6
- state_read: bfloat16 [20480, 128], P('seq'), may hold values from -1.5 to 1.5
- conv_feat: float32 [4, 8192], P(None, 'head'), may hold values from -3 to 3
- conv_state: float32 [4, 256], replicated, may hold values from -3 to 3
- log_decay: float32 [20480, 128], P('seq', 'head'), may hold values from -0.81 to 0, as said below
- skip_weight: float32 [128], P('head'), may hold values from 0.5 to 2
- norm_gain: float32 [8192], P('head'), may hold values from 0.5 to 1.5
Outputs:
- mixed_out: bfloat16 [20480, 8192], P('seq', 'head')
The draws below stay inside these ranges and needn't reach their ends.
Inputs may be any that keep to these rules, and one draw needn't show every extreme that they name: `log_decay`: every log decay is strictly negative.
All inputs are finite; a program needn't handle non-finite values.
Results may differ from the reference program's by a relative error of at most 0.0094.
Values may be sent and summed in bfloat16 or wider, within the bound.
No kernel may reach another device: no remote copies, remote signals or barrier semaphores. Data moves between devices by JAX's collectives and lax.ppermute only.
A program may use at most 128 MiB of HBM per device.

```python
import math
import jax
import jax.numpy as jnp
from jax import lax

MIXER_HEADS = 128
HEAD_DIM = 64
STATE = 128
CONV = 4
BLOCK = 256
TOK_DEV = 2560
SEQUENCE_TOKENS = 20480
CHANNELS = 8192


def draw_features(key, part):
    key_base, key_head, key_row = jax.random.split(key, 3)
    head_ramp = jnp.arange(MIXER_HEADS, dtype=jnp.float32) / (MIXER_HEADS - 1)
    head_scale = jnp.exp(head_ramp * math.log(10.0)) * jax.random.uniform(key_head, (MIXER_HEADS,), jnp.float32, 0.8, 1.25)
    base_draw = jax.random.truncated_normal(key_base, -6.0, 6.0, (SEQUENCE_TOKENS, MIXER_HEADS, HEAD_DIM), jnp.float32)
    row_scale = jnp.exp(jax.random.uniform(key_row, (SEQUENCE_TOKENS, 1, 1), jnp.float32, 0.0, math.log(10.0)))
    values = base_draw * head_scale[None, :, None] * row_scale / 10.0
    return values.reshape(SEQUENCE_TOKENS, MIXER_HEADS * HEAD_DIM).astype(jnp.bfloat16)


def draw_log_decay(key, part):
    random_keys = jax.random.split(key, 7)
    fraction = 0.5
    is_fast = jax.random.uniform(random_keys[0], (MIXER_HEADS,), jnp.float32) < fraction
    fast_rate = jnp.exp(jax.random.uniform(random_keys[1], (MIXER_HEADS,), jnp.float32, math.log(1.0 / 50.0), math.log(1.0 / 20.0)))
    slow_rate = jax.random.uniform(random_keys[2], (MIXER_HEADS,), jnp.float32, 0.15, 0.5) / SEQUENCE_TOKENS
    base_rate = jnp.where(is_fast, fast_rate, slow_rate)
    device_blocks = SEQUENCE_TOKENS // TOK_DEV
    block_factor = jnp.exp(jax.random.uniform(random_keys[3], (device_blocks, 1, MIXER_HEADS), jnp.float32, math.log(0.5), math.log(1.5)))
    roughness = jax.random.uniform(random_keys[4], (device_blocks, TOK_DEV, MIXER_HEADS), jnp.float32, 0.5, 1.5)
    constant_level = -(base_rate[None, None, :] * block_factor * roughness).reshape(SEQUENCE_TOKENS, MIXER_HEADS)
    spike_locations = jax.random.randint(random_keys[5], (2,), 0, SEQUENCE_TOKENS)
    spike_height = jax.random.uniform(random_keys[6], (1, MIXER_HEADS), jnp.float32, 0.22, 0.69)
    token_places = jnp.arange(SEQUENCE_TOKENS, dtype=jnp.int32)
    inside_spike = jnp.any(token_places[:, None] == spike_locations[None, :], axis=1)
    return constant_level - jnp.where(inside_spike[:, None], spike_height, 0.0)


def levels(stream_key, extent, shards, low, top_value):
    def one(axis_at, parts):
        draws = jax.random.uniform(jax.random.fold_in(jax.random.fold_in(stream_key, 6), axis_at), (parts,), jnp.float32, low / len(shards), top_value / len(shards))
        return jnp.repeat(jnp.exp(draws), extent[axis_at] // parts).reshape((-1,) + (1,) * (len(extent) - axis_at - 1))

    gain = one(*shards[0])
    for cut in shards[1:]:
        gain = gain * one(*cut)
    return gain


def scatter_about(stream_key, extent, width, most, shards=(), kind=jnp.bfloat16):
    gain = levels(stream_key, extent, shards, -0.22, 0.18) if shards else 1.0
    values = jax.random.normal(stream_key, extent, jnp.float32) * width * gain
    return jnp.minimum(jnp.maximum(values, -most), most).astype(kind)


def setup_inputs(seed: int = 0) -> dict:
    splits = jax.random.split(jax.random.key(seed), 9)
    return {
        "features": draw_features(jax.random.fold_in(splits[8], 71), 0),
        "state_write": scatter_about(splits[1], (SEQUENCE_TOKENS, STATE), 1.0, 6.0, ((0, 8),)),
        "state_read": scatter_about(splits[2], (SEQUENCE_TOKENS, STATE), 0.25, 1.5, ((0, 8),)),
        "conv_feat": scatter_about(splits[3], (CONV, CHANNELS), CONV ** -0.5, 3.0, ((1, 4),), jnp.float32),
        "conv_state": scatter_about(splits[4], (CONV, 2 * STATE), CONV ** -0.5, 3.0, (), jnp.float32),
        "log_decay": draw_log_decay(jax.random.fold_in(splits[8], 71), 0),
        "skip_weight": jnp.clip(jnp.exp(math.log(2.0) - 1.3862944 * jax.random.uniform(splits[6], (MIXER_HEADS,), jnp.float32) ** levels(splits[6], (MIXER_HEADS,), ((0, 4),), -0.2, 0.2)), 0.5, 2.0),
        "norm_gain": jnp.clip(1.0 + 0.1 * jax.random.normal(splits[7], (CHANNELS,), jnp.float32), 0.5, 1.5),
    }


def conv_silu(extended, kernel_taps, length):
    summed = extended[0:length].astype(jnp.float32) * kernel_taps[0]
    for place in range(1, kernel_taps.shape[0]):
        summed = summed + extended[place:place + length].astype(jnp.float32) * kernel_taps[place]
    return jax.nn.silu(summed).astype(jnp.bfloat16)

def reference(features, state_write, state_read, conv_feat, conv_state, log_decay, skip_weight, norm_gain):
    margin = CONV - 1
    feat_conv = conv_silu(jnp.concatenate([jnp.zeros((margin, CHANNELS), jnp.bfloat16), features], axis=0), conv_feat, SEQUENCE_TOKENS)
    joined = jnp.concatenate([jnp.zeros((margin, 2 * STATE), jnp.bfloat16), jnp.concatenate([state_write, state_read], axis=1)], axis=0)
    state_conv = conv_silu(joined, conv_state, SEQUENCE_TOKENS)
    groups = SEQUENCE_TOKENS // BLOCK
    sliced = (feat_conv.reshape(groups, BLOCK, MIXER_HEADS, HEAD_DIM), state_conv[:, :STATE].reshape(groups, BLOCK, STATE), state_conv[:, STATE:].reshape(groups, BLOCK, STATE), log_decay.reshape(groups, BLOCK, MIXER_HEADS))
    causal_mask = jnp.tril(jnp.ones((BLOCK, BLOCK), dtype=bool))

    def advance(carried, pieces):
        feature_rows, write_rows, read_rows, decay_rows = pieces
        cumul_rows = jnp.cumsum(decay_rows, axis=0)
        block_total = cumul_rows[-1]
        scales = jnp.sqrt(-jnp.expm1(2.0 * decay_rows))
        scores = jnp.dot(read_rows, write_rows.T, preferred_element_type=jnp.float32)
        cum_heads = cumul_rows.T
        decay_gaps = jnp.where(causal_mask[None], cum_heads[:, :, None] - cum_heads[:, None, :], -1e+30)
        mixing = (scores[None] * jnp.exp(decay_gaps) * scales.T[:, None, :]).astype(jnp.bfloat16)
        mixing = lax.optimization_barrier(mixing).astype(jnp.float32)
        feat_wide = feature_rows.astype(jnp.float32)
        within = jnp.einsum('hts,shp->thp', mixing, feat_wide)
        start_bf = lax.optimization_barrier(carried.astype(jnp.bfloat16)).astype(jnp.float32)
        from_state = jnp.einsum('tn,hpn->thp', read_rows.astype(jnp.float32), start_bf) * jnp.exp(cumul_rows)[:, :, None]
        mixed = within + from_state + skip_weight[None, :, None] * feat_wide
        decayed = ((jnp.exp(block_total[None, :] - cumul_rows) * scales)[:, :, None] * feat_wide).astype(jnp.bfloat16)
        decayed = lax.optimization_barrier(decayed).astype(jnp.float32)
        contrib = jnp.einsum('qn,qhp->hpn', write_rows.astype(jnp.float32), decayed)
        following = jnp.exp(block_total)[:, None, None] * carried + contrib
        flat = mixed.reshape(BLOCK, CHANNELS)
        meansq = lax.optimization_barrier(jnp.mean(flat * flat, axis=1, keepdims=True))
        normed = (flat * lax.rsqrt(meansq + 1e-05) * norm_gain[None, :]).astype(jnp.bfloat16)
        return (following, normed)
    final_state, outputs = lax.scan(advance, jnp.zeros((MIXER_HEADS, HEAD_DIM, STATE), jnp.float32), sliced)
    return outputs.reshape(SEQUENCE_TOKENS, CHANNELS)
```

```python
import functools

import jax
import jax.numpy as jnp
from jax import lax
from jax.experimental import pallas as pl
from jax.experimental.pallas import tpu as pltpu
from jax.sharding import PartitionSpec as P

EPSILON = 1e-05
SUB = 128
ROWS = 256
WIDE = 256
GROUP = 4
F32 = jnp.float32
BF16 = jnp.bfloat16
HIGHEST = lax.Precision.HIGHEST
MIB = 1 << 20

VMEM = pl.BlockSpec(memory_space=pltpu.VMEM)
SMEM = pl.BlockSpec(memory_space=pltpu.SMEM)
ANY = pl.BlockSpec(memory_space=pl.ANY)


def dot(a, b):
    return jnp.dot(a, b, preferred_element_type=F32)


def exact_dot(a, b):
    return jnp.dot(a, b, preferred_element_type=F32, precision=HIGHEST)


def iota(shape, dim):
    return lax.broadcasted_iota(jnp.int32, shape, dim)


def split_pair(value, low):
    high = value.astype(BF16).astype(F32)
    return jnp.where(low, value - high, high).astype(BF16)


def decay_kernel(heads, ld_ref, skip_ref, ab_ref, fe_ref, rows_ref, first_ref, second_ref, cum_ref, sc_ref):
    tokens = ld_ref.shape[0]
    channels = rows_ref.shape[1]
    blocks = tokens // SUB
    width = 4 * heads
    dim_shift = (channels // heads).bit_length() - 1
    lower = (iota((SUB, SUB), 0) >= iota((SUB, SUB), 1)).astype(F32)
    lane = iota((SUB, width), 1)
    low = (lane & heads) != 0
    second = lane >= 2 * heads
    totals, refs = [], []
    for b in range(blocks):
        at = pl.ds(b * SUB, SUB)
        part = ld_ref[at, :]
        decay = jnp.concatenate([part] * 4, axis=1)
        cumul = exact_dot(lower, decay)
        y = 2.0 * decay
        series = -y * (1.0 + y * (1 / 2) * (1.0 + y * (1 / 3) * (1.0 + y * (1 / 4) * (1.0 + y * (1 / 5)))))
        scale = jnp.sqrt(jnp.where(y > -0.1, series, 1.0 - jnp.exp(y)))
        ref = cumul[SUB // 2 - 1 : SUB // 2]
        gap = cumul - ref
        value = jnp.exp(jnp.where(second, -gap, gap)) * jnp.where(second, scale, 1.0)
        ab_ref[at, :] = split_pair(value, low)
        cum_ref[at, :] = cumul
        sc_ref[at, :] = scale
        totals.append(cumul[SUB - 1 : SUB])
        refs.append(ref)
    zero = jnp.zeros_like(totals[0])
    before = [zero]
    for b in range(blocks - 1):
        before.append(before[-1] + totals[b])
    after = [zero] * blocks
    for b in range(blocks - 2, -1, -1):
        after[b] = after[b + 1] + totals[b + 1]
    for b in range(blocks):
        at = pl.ds(b * SUB, SUB)
        cumul = cum_ref[at, :]
        power = jnp.where(second, cumul + before[b], (totals[b] - cumul) + after[b])
        value = jnp.exp(power) * jnp.where(second, 1.0, sc_ref[at, :])
        fe_ref[at, :] = split_pair(value, low)
    rows = [jnp.exp(totals[b] - refs[b] + refs[b + 1]) for b in range(blocks - 1)] + [zero]
    rows.append(jnp.exp(before[-1] + totals[-1]))
    rows.append(jnp.concatenate([skip_ref[...]] * 4, axis=1))
    rows += [zero] * (rows_ref.shape[0] - len(rows))
    head_of = lax.shift_right_logical(iota((width, channels), 1), dim_shift)
    row = iota((width, channels), 0)
    rows_ref[...] = exact_dot(jnp.concatenate(rows, axis=0), (row == head_of).astype(F32))
    match = (row & (heads - 1)) == head_of
    first_ref[...] = (match & (row < 2 * heads)).astype(F32).astype(BF16)
    second_ref[...] = (match & (row >= 2 * heads)).astype(F32).astype(BF16)


def decay_prep(log_decay, skip_weight, channels):
    tokens, heads = log_decay.shape
    blocks = tokens // SUB
    rows = -(-(blocks + 2) // 8) * 8
    width = 4 * heads
    return pl.pallas_call(
        functools.partial(decay_kernel, heads),
        in_specs=[VMEM, VMEM],
        out_specs=[VMEM] * 5,
        out_shape=[
            pltpu.VMEM((tokens, width), BF16),
            pltpu.VMEM((tokens, width), BF16),
            pltpu.VMEM((rows, channels), F32),
            pltpu.VMEM((width, channels), BF16),
            pltpu.VMEM((width, channels), BF16),
        ],
        scratch_shapes=[pltpu.VMEM((tokens, width), F32), pltpu.VMEM((tokens, width), F32)],
        compiler_params=pltpu.CompilerParams(vmem_limit_bytes=12 * MIB),
        cost_estimate=pl.CostEstimate(flops=10**9, bytes_accessed=5 * 10**6, transcendentals=10**6),
        name="decay_prep",
    )(log_decay, skip_weight.reshape(1, heads))


def conv_silu(ref, taps, cols):
    rows = ref.shape[0] - 8
    total = None
    for k in range(4):
        term = ref[pl.ds(5 + k, rows), cols] * (0.5 * taps[k : k + 1])
        total = term if total is None else total + term
    return total + total * jnp.tanh(total)


def conv_kernel(
    place_ref, halo_ref, feat_ref, write_ref, read_ref, taps_ref, state_taps_ref, fe_ref, first_ref, rows_ref,
    *refs,
):
    *x_refs, wt_ref, c_ref, msg_ref, buf, state_buf, carry = refs
    step = pl.program_id(0)
    rows = feat_ref.shape[0]
    channels = feat_ref.shape[1]
    state = write_ref.shape[1]
    quarter = channels // GROUP
    blocks = x_refs[0].shape[0] // SUB

    @pl.when(step == 0)
    def _():
        halo = halo_ref[...].astype(F32)[8:16]
        buf[0:8, :] = halo[:, :channels]
        state_buf[0:8, :] = halo[:, channels:]
        carry[...] = jnp.zeros_like(carry)

    @pl.when(step > 0)
    def _():
        buf[0:8, :] = buf[rows : rows + 8, :]
        state_buf[0:8, :] = state_buf[rows : rows + 8, :]

    state_buf[8:, :state] = write_ref[...].astype(F32)
    state_buf[8:, state:] = read_ref[...].astype(F32)
    conv = conv_silu(state_buf, state_taps_ref[...], slice(None))
    c_ref[...] = conv[:, state:].astype(BF16)
    wt = conv[:, :state].T.astype(BF16)
    wt_ref[...] = wt
    here = pl.ds(pl.multiple_of(step * rows, rows), rows)
    fe = fe_ref[...]
    homes = [(ref, n) for ref in x_refs for n in range(ref.shape[1] // WIDE)]
    for chunk, (x_ref, n) in enumerate(homes):
        cols = pl.ds(chunk * WIDE, WIDE)
        buf[8:, cols] = feat_ref[:, cols].astype(F32)
        x = conv_silu(buf, taps_ref[:, cols], cols)
        x_ref[here, pl.ds(n * WIDE, WIDE)] = x
        decayed = (x * dot(fe, first_ref[:, cols])).astype(BF16)
        q, off = divmod(chunk * WIDE, quarter)
        inside = pl.ds(off, WIDE)
        carry[q, :, inside] += dot(wt, decayed)

    @pl.when(step == pl.num_programs(0) - 1)
    def _():
        place = place_ref[0]
        for q in range(GROUP):
            slot = lax.bitwise_xor(place, q)
            msg_ref[slot, 0:state, :] = carry[q].astype(BF16)
            decay = jnp.broadcast_to(rows_ref[blocks : blocks + 1, q * quarter : (q + 1) * quarter], (16, quarter))
            msg_ref[slot, state:, :] = split_pair(decay, iota((16, quarter), 0) == 1)


def conv_states(parts, place, halo, features, state_write, state_read, conv_feat, conv_state, fe, first, rows):
    tokens, channels = features.shape
    state = state_write.shape[1]
    quarter = channels // GROUP
    width = fe.shape[1]
    return pl.pallas_call(
        conv_kernel,
        grid=(tokens // ROWS,),
        in_specs=[
            SMEM,
            VMEM,
            pl.BlockSpec((ROWS, channels), lambda i: (i, 0)),
            pl.BlockSpec((ROWS, state), lambda i: (i, 0)),
            pl.BlockSpec((ROWS, state), lambda i: (i, 0)),
            VMEM,
            VMEM,
            pl.BlockSpec((ROWS, width), lambda i: (i, 0)),
            VMEM,
            VMEM,
        ],
        out_specs=[VMEM] * len(parts)
        + [
            pl.BlockSpec((state, ROWS), lambda i: (0, i)),
            pl.BlockSpec((ROWS, state), lambda i: (i, 0)),
            VMEM,
        ],
        out_shape=[pltpu.VMEM((tokens, part), F32) for part in parts]
        + [
            pltpu.VMEM((state, tokens), BF16),
            pltpu.VMEM((tokens, state), BF16),
            jax.ShapeDtypeStruct((GROUP, state + 16, quarter), BF16),
        ],
        scratch_shapes=[
            pltpu.VMEM((ROWS + 8, channels), F32),
            pltpu.VMEM((ROWS + 8, 2 * state), F32),
            pltpu.VMEM((GROUP, state, quarter), F32),
        ],
        compiler_params=pltpu.CompilerParams(vmem_limit_bytes=12 * MIB),
        cost_estimate=pl.CostEstimate(flops=10**10, bytes_accessed=10**7, transcendentals=10**6),
        name="conv_states",
    )(place, halo, features, state_write, state_read, conv_feat, conv_state, fe, first, rows)


def scores_kernel(c_ref, wt_ref, sc_ref):
    state = c_ref.shape[1]
    keep = iota((SUB, SUB), 0) >= iota((SUB, SUB), 1)

    for b in range(c_ref.shape[0] // SUB):
        at = pl.ds(b * SUB, SUB)
        c = c_ref[at, :]
        sc_ref[at, 0:SUB] = jnp.where(keep, dot(c, wt_ref[:, at]), 0.0).astype(BF16)
        sc_ref[at, SUB : SUB + state] = c


def block_scores(c, wt):
    tokens, state = c.shape
    return pl.pallas_call(
        scores_kernel,
        in_specs=[VMEM, VMEM],
        out_specs=VMEM,
        out_shape=pltpu.VMEM((tokens, SUB + state), BF16),
        compiler_params=pltpu.CompilerParams(vmem_limit_bytes=12 * MIB),
        cost_estimate=pl.CostEstimate(flops=10**9, bytes_accessed=2 * 10**6, transcendentals=0),
        name="block_scores",
    )(c, wt)


def within_kernel(offset, _, x_ref, sc_ref, wt_ref, ab_ref, first_ref, second_ref, rows_ref, out_ref, start):
    blocks = x_ref.shape[0] // SUB
    start[...] = jnp.zeros_like(start)

    def block(b, _):
        at = pl.ds(pl.multiple_of(b * SUB, SUB), SUB)
        ab = ab_ref[at, :]
        sc = sc_ref[at, :]
        wt = wt_ref[:, at]
        for n in range(x_ref.shape[1] // WIDE):
            cols = pl.ds(offset + n * WIDE, WIDE)
            here = pl.ds(n * WIDE, WIDE)
            x = x_ref[at, here]
            bx = (x * dot(ab, second_ref[:, cols])).astype(BF16)
            now = start[n]
            inner = dot(sc, jnp.concatenate([bx, now.astype(BF16)], axis=0))
            out_ref[at, here] = dot(ab, first_ref[:, cols]) * inner + rows_ref[blocks + 1 : blocks + 2, cols] * x
            start[n] = rows_ref[pl.ds(b, 1), cols] * (now + dot(wt, bx))
        return 0

    lax.fori_loop(0, blocks, block, 0)


def within(offset, after, x, sc, wt, ab, first, second, rows):
    tokens, part = x.shape
    state = wt.shape[0]
    return pl.pallas_call(
        functools.partial(within_kernel, offset),
        in_specs=[ANY] + [VMEM] * 7,
        out_specs=VMEM,
        out_shape=pltpu.VMEM((tokens, part), F32),
        scratch_shapes=[pltpu.VMEM((part // WIDE, state, WIDE), F32)],
        compiler_params=pltpu.CompilerParams(vmem_limit_bytes=8 * MIB),
        cost_estimate=pl.CostEstimate(flops=2 * 10**9, bytes_accessed=16 * tokens * part, transcendentals=0),
        name="within",
    )(after, x, sc, wt, ab, first, second, rows)


def group_kernel(place_ref, msg_ref, r1_ref, r2_ref, r3_ref, total_ref, prefix_ref, decay_ref, held):
    place = place_ref[0]
    state = prefix_ref.shape[1]
    held[place] = msg_ref[0]
    for k, ref in enumerate((r1_ref, r2_ref, r3_ref)):
        held[lax.bitwise_xor(place, k + 1)] = ref[...]
    sofar = jnp.zeros(prefix_ref.shape[1:], F32)
    decays = jnp.ones((1, sofar.shape[1]), F32)
    for j in range(GROUP):
        tail = held[j, state:, :].astype(F32)
        decay = tail[0:1] + tail[1:2]
        prefix_ref[j] = sofar
        decay_ref[j : j + 1, :] = decays
        sofar = decay * sofar + held[j, 0:state, :].astype(F32)
        decays = decay * decays
    total_ref[0:state, :] = sofar.astype(BF16)
    wide = jnp.broadcast_to(decays, (16, decays.shape[1]))
    total_ref[state:, :] = split_pair(wide, iota(wide.shape, 0) == 1)


def group_prefix(place, msg, received):
    _, rows, quarter = msg.shape
    state = rows - 16
    return pl.pallas_call(
        group_kernel,
        in_specs=[SMEM] + [VMEM] * 4,
        out_specs=[VMEM] * 3,
        out_shape=[
            jax.ShapeDtypeStruct((rows, quarter), BF16),
            pltpu.VMEM((GROUP, state, quarter), F32),
            pltpu.VMEM((8, quarter), F32),
        ],
        scratch_shapes=[pltpu.VMEM((GROUP, rows, quarter), BF16)],
        compiler_params=pltpu.CompilerParams(vmem_limit_bytes=12 * MIB),
        name="group_prefix",
    )(place, msg, *received)


def spread_kernel(place_ref, prefix_ref, decay_ref, carried_ref, *out_refs):
    place = place_ref[0]
    state = prefix_ref.shape[1]
    carried = carried_ref[0:state, :].astype(F32)
    for k, ref in enumerate(out_refs):
        j = lax.bitwise_xor(place, k)
        ref[...] = (prefix_ref[j] + decay_ref[pl.ds(j, 1), :] * carried).astype(BF16)


def spread(place, prefix, decay, carried):
    _, state, quarter = prefix.shape
    return pl.pallas_call(
        spread_kernel,
        in_specs=[SMEM] + [VMEM] * 3,
        out_specs=[VMEM] * GROUP,
        out_shape=[jax.ShapeDtypeStruct((state, quarter), BF16)] * GROUP,
        compiler_params=pltpu.CompilerParams(vmem_limit_bytes=12 * MIB),
        name="spread",
    )(place, prefix, decay, carried)


def state_kernel(count, place_ref, c_ref, fe_ref, second_ref, s0, s1, s2, s3, *refs):
    m_refs, out_refs, (sq_ref, start) = refs[:count], refs[count : 2 * count], refs[2 * count :]
    place = place_ref[0]
    tokens = c_ref.shape[0]
    quarter = s0.shape[1]
    for k, ref in enumerate((s0, s1, s2, s3)):
        start[lax.bitwise_xor(place, k)] = ref[...]
    homes = [(m, o, n) for m, o in zip(m_refs, out_refs) for n in range(m.shape[1] // WIDE)]

    def block(b, _):
        at = pl.ds(pl.multiple_of(b * SUB, SUB), SUB)
        c = c_ref[at, :]
        fe = fe_ref[at, :]
        squares = jnp.zeros((SUB, 128), F32)
        for chunk, (m_ref, out_ref, n) in enumerate(homes):
            cols = pl.ds(chunk * WIDE, WIDE)
            here = pl.ds(n * WIDE, WIDE)
            q, off = divmod(chunk * WIDE, quarter)
            value = m_ref[at, here] + dot(fe, second_ref[:, cols]) * dot(c, start[q, :, off : off + WIDE])
            out_ref[at, here] = value
            for lane in range(0, WIDE, 128):
                piece = value[:, lane : lane + 128]
                squares = squares + piece * piece
        sq_ref[pl.ds(b, 1), :] = jnp.sum(squares.T, axis=0, keepdims=True)
        return 0

    lax.fori_loop(0, tokens // SUB, block, 0)


def add_states(place, ms, c, fe, second, pieces):
    tokens, state = c.shape
    quarter = pieces[0].shape[1]
    blocks = tokens // SUB
    return pl.pallas_call(
        functools.partial(state_kernel, len(ms)),
        in_specs=[SMEM] + [VMEM] * (3 + GROUP + len(ms)),
        out_specs=[VMEM] * (len(ms) + 1),
        out_shape=[pltpu.VMEM(m.shape, F32) for m in ms] + [jax.ShapeDtypeStruct((blocks, SUB), F32)],
        scratch_shapes=[pltpu.VMEM((GROUP, state, quarter), BF16)],
        compiler_params=pltpu.CompilerParams(vmem_limit_bytes=8 * MIB),
        name="add_states",
    )(place, c, fe, second, *pieces, *ms)


def norm_kernel(size, count, gain_ref, *refs):
    m_refs, sq_refs, out_ref = refs[:count], refs[count:-1], refs[-1]
    step = pl.program_id(0)
    rows = out_ref.shape[0]
    homes = [(m, n) for m in m_refs for n in range(m.shape[1] // 128)]
    for sub in range(rows // SUB):
        b = step * (rows // SUB) + sub
        total = sq_refs[0][pl.ds(b, 1), :]
        for ref in sq_refs[1:]:
            total = total + ref[pl.ds(b, 1), :]
        scale = lax.rsqrt(total * (1.0 / size) + EPSILON)
        scale = jnp.broadcast_to(scale, (SUB, SUB)).T
        at = pl.ds(pl.multiple_of(b * SUB, SUB), SUB)
        for tile, (m_ref, n) in enumerate(homes):
            cols = pl.ds(tile * 128, 128)
            value = m_ref[at, pl.ds(n * 128, 128)] * scale * gain_ref[:, cols]
            out_ref[pl.ds(sub * SUB, SUB), cols] = value.astype(BF16)


def norm(size, ms, gain, squares):
    tokens = ms[0].shape[0]
    channels = gain.shape[0]
    rows = 512
    return pl.pallas_call(
        functools.partial(norm_kernel, size, len(ms)),
        grid=(tokens // rows,),
        in_specs=[VMEM] * (1 + len(ms) + len(squares)),
        out_specs=pl.BlockSpec((rows, channels), lambda i: (i, 0)),
        out_shape=jax.ShapeDtypeStruct((tokens, channels), BF16),
        compiler_params=pltpu.CompilerParams(vmem_limit_bytes=8 * MIB),
        name="norm",
    )(gain.reshape(1, channels), *ms, *squares)


def later(value, steps):
    count = lax.axis_size("seq")
    return lax.ppermute(value, "seq", [(i, i + steps) for i in range(count - steps)])


def partner(value, axis, mask):
    return lax.ppermute(value, axis, [(i, i ^ mask) for i in range(lax.axis_size(axis))])


def group_carry(total):
    groups = lax.axis_size("seq") // GROUP
    carried = later(total, GROUP)
    state = total.shape[0] - 16
    reach = 1
    while reach < groups - 1:
        got = later(carried, reach * GROUP).astype(F32)
        mine = carried.astype(F32)
        decay = mine[state : state + 1] + mine[state + 1 : state + 2]
        got_decay = got[state : state + 1] + got[state + 1 : state + 2]
        values = mine[:state] + decay * got[:state]
        both = decay * got_decay
        high = both.astype(BF16)
        rest = (both - high.astype(F32)).astype(BF16)
        carried = jnp.concatenate(
            [values.astype(BF16), high, rest, jnp.zeros((14, both.shape[1]), BF16)], axis=0
        )
        reach *= 2
    return carried


def on_device(
    features, state_write, state_read, conv_feat, conv_state, log_decay, skip_weight, norm_gain
):
    tokens, channels = features.shape
    place = lax.rem(lax.axis_index("seq"), GROUP).astype(jnp.int32).reshape(1)
    tail = jnp.concatenate([features[-16:], state_write[-16:], state_read[-16:]], axis=1)
    halo = later(tail, 1)
    ab, fe, rows, first, second = decay_prep(log_decay, skip_weight, channels)
    chunks = channels // WIDE
    cuts = [0, (3 * chunks) // 8 * WIDE, (5 * chunks) // 8 * WIDE, channels]
    parts = [cuts[n + 1] - cuts[n] for n in range(3)]
    *xs, wt, c, msg = conv_states(
        parts, place, halo, features, state_write, state_read, conv_feat, conv_state, fe, first, rows
    )
    received = [partner(msg[k], "seq", k) for k in range(1, GROUP)]
    sc = block_scores(c, wt)
    shared = (sc, wt, ab, first, second, rows)
    ms = [within(cuts[0], place, xs[0], *shared)]
    total, prefix, decay = group_prefix(place, msg, received)
    carried = group_carry(total)
    ms.append(within(cuts[1], total, xs[1], *shared))
    pieces = spread(place, prefix, decay, carried)
    starts = [pieces[0]] + [partner(pieces[k], "seq", k) for k in range(1, GROUP)]
    ms.append(within(cuts[2], pieces[0], xs[2], *shared))
    *ms, squares = add_states(place, ms, c, fe, second, starts)
    others = [partner(squares, "head", k) for k in range(1, lax.axis_size("head"))]
    size = channels * lax.axis_size("head")
    return norm(size, ms, norm_gain, [squares] + others)


def solution(mesh):
    placed = (
        P("seq", "head"),
        P("seq", None),
        P("seq", None),
        P(None, "head"),
        P(),
        P("seq", "head"),
        P("head"),
        P("head"),
    )
    return jax.shard_map(
        on_device, mesh=mesh, in_specs=placed, out_specs=P("seq", "head"), check_vma=False
    )
```

```python
import functools

import jax
import jax.numpy as jnp
from jax import lax
from jax.experimental import pallas as pl
from jax.experimental.pallas import tpu as pltpu
from jax.sharding import PartitionSpec as P

EPSILON = 1e-05
SUB = 128
WIDE = 256
ROWS = 256
RING = 4
GROUP = 4
UNROLL = 4
F32 = jnp.float32
BF16 = jnp.bfloat16
HIGHEST = lax.Precision.HIGHEST
MIB = 1 << 20

VMEM = pl.BlockSpec(memory_space=pltpu.VMEM)
SMEM = pl.BlockSpec(memory_space=pltpu.SMEM)
ANY = pl.BlockSpec(memory_space=pl.ANY)


def dot(a, b):
    return jnp.dot(a, b, preferred_element_type=F32)


def exact_dot(a, b):
    return jnp.dot(a, b, preferred_element_type=F32, precision=HIGHEST)


def iota(shape, dim):
    return lax.broadcasted_iota(jnp.int32, shape, dim)


def split_pair(value, low):
    high = value.astype(BF16).astype(F32)
    return jnp.where(low, value - high, high).astype(BF16)


def per_head(table, group, heads, head_dim, tile):
    shift = head_dim.bit_length() - 1
    lane = lax.shift_right_logical(iota(table.shape, 1), shift)
    return jnp.take_along_axis(table, lane + (group * heads + tile * (128 // head_dim)), axis=1)


def decay_kernel(heads, ld_ref, skip_ref, table_ref, pair_ref, rows_ref, first_ref, second_ref, cum_ref, sc_ref):
    tokens = ld_ref.shape[0]
    channels = rows_ref.shape[1]
    blocks = tokens // SUB
    dim_shift = (channels // heads).bit_length() - 1
    copies = 128 // heads
    lower = (iota((SUB, SUB), 0) >= iota((SUB, SUB), 1)).astype(F32)
    lane = iota((SUB, 128), 1)
    totals, refs = [], []
    for b in range(blocks):
        at = pl.ds(b * SUB, SUB)
        decay = jnp.concatenate([ld_ref[at, :]] * copies, axis=1)
        cumul = exact_dot(lower, decay)
        y = 2.0 * decay
        series = -y * (1.0 + y * (1 / 2) * (1.0 + y * (1 / 3) * (1.0 + y * (1 / 4) * (1.0 + y * (1 / 5)))))
        cum_ref[at, :] = cumul
        sc_ref[at, :] = jnp.sqrt(jnp.where(y > -0.1, series, 1.0 - jnp.exp(y)))
        totals.append(cumul[SUB - 1 : SUB])
        refs.append(cumul[SUB // 2 - 1 : SUB // 2])
    zero = jnp.zeros_like(totals[0])
    before = [zero]
    for b in range(blocks - 1):
        before.append(before[-1] + totals[b])
    after = [zero] * blocks
    for b in range(blocks - 2, -1, -1):
        after[b] = after[b + 1] + totals[b + 1]
    row_lane = iota((1, 128), 1)
    negative = (row_lane >= heads) & (row_lane < 3 * heads)
    scaled = (lane >= heads) & (lane < 3 * heads)
    low = (lane & heads) != 0
    for b in range(blocks):
        at = pl.ds(b * SUB, SUB)
        cumul = cum_ref[at, :]
        base = jnp.where(
            row_lane < heads,
            -refs[b],
            jnp.where(row_lane < 2 * heads, refs[b], jnp.where(row_lane < 3 * heads, totals[b], before[b])),
        )
        power = base + jnp.where(negative, -cumul, cumul) + jnp.where(negative & (row_lane >= 2 * heads), after[b], 0.0)
        table_ref[at, :] = jnp.exp(power) * jnp.where(scaled, sc_ref[at, :], 1.0)
        value = jnp.exp(cumul + jnp.where(row_lane < 2 * heads, -refs[b], before[b]))
        pair_ref[at, :] = split_pair(value, low)
    rows = [jnp.exp(totals[b] - refs[b] + refs[b + 1]) for b in range(blocks - 1)] + [zero]
    rows.append(jnp.exp(before[-1] + totals[-1]))
    rows.append(jnp.concatenate([skip_ref[...]] * copies, axis=1))
    rows += [zero] * (rows_ref.shape[0] - len(rows))
    head_of = lax.shift_right_logical(iota((128, channels), 1), dim_shift)
    row = iota((128, channels), 0)
    rows_ref[...] = exact_dot(jnp.concatenate(rows, axis=0), (row == head_of).astype(F32))
    match = (row & (heads - 1)) == head_of
    first_ref[...] = (match & (row < 2 * heads)).astype(F32).astype(BF16)
    second_ref[...] = (match & (row >= 2 * heads) & (row < 4 * heads)).astype(F32).astype(BF16)


def decay_prep(log_decay, skip_weight, channels):
    tokens, heads = log_decay.shape
    blocks = tokens // SUB
    rows = -(-(blocks + 2) // 8) * 8
    return pl.pallas_call(
        functools.partial(decay_kernel, heads),
        in_specs=[VMEM, VMEM],
        out_specs=[VMEM] * 5,
        out_shape=[
            pltpu.VMEM((tokens, 128), F32),
            pltpu.VMEM((tokens, 128), BF16),
            pltpu.VMEM((rows, channels), F32),
            pltpu.VMEM((128, channels), BF16),
            pltpu.VMEM((128, channels), BF16),
        ],
        scratch_shapes=[pltpu.VMEM((tokens, 128), F32), pltpu.VMEM((tokens, 128), F32)],
        compiler_params=pltpu.CompilerParams(vmem_limit_bytes=8 * MIB),
        cost_estimate=pl.CostEstimate(flops=10**9, bytes_accessed=5 * 10**6, transcendentals=10**6),
        name="decay_prep",
    )(log_decay, skip_weight.reshape(1, heads))


def tail_kernel(feat_ref, write_ref, read_ref, out_ref):
    channels = feat_ref.shape[1]
    state = write_ref.shape[1]
    out_ref[:, :channels] = feat_ref[...]
    out_ref[:, channels : channels + state] = write_ref[...]
    out_ref[:, channels + state :] = read_ref[...]


def tail_rows(features, state_write, state_read):
    tokens, channels = features.shape
    state = state_write.shape[1]
    last = tokens // 16 - 1
    return pl.pallas_call(
        tail_kernel,
        grid=(1,),
        in_specs=[pl.BlockSpec((16, width), lambda i: (last, 0)) for width in (channels, state, state)],
        out_specs=pl.BlockSpec((16, channels + 2 * state), lambda i: (0, 0)),
        out_shape=jax.ShapeDtypeStruct((16, channels + 2 * state), BF16),
        compiler_params=pltpu.CompilerParams(vmem_limit_bytes=2 * MIB),
        name="tail_rows",
    )(*map(in_hbm, (features, state_write, state_read)))


def in_hbm(value):
    return pltpu.with_memory_space_constraint(value, pltpu.HBM)


def conv_silu(ref, base, rows, taps):
    total = None
    for k in range(4):
        term = ref[pl.ds(base + 5 + k, rows), :] * taps[k : k + 1]
        total = term if total is None else total + term
    return total + total * jnp.tanh(total)


def conv_kernel(
    heads, count, place_ref, halo_ref, feat_ref, write_ref, read_ref, taps_ref, state_taps_ref, table_ref, rows_ref,
    *refs,
):
    *x_refs, wt_ref, c_ref, msg_ref, carry, feat_ring, write_ring, read_ring, sems = refs[:-count]
    bufs = refs[-count:]
    tokens, channels = feat_ref.shape
    head_dim = channels // heads
    state = write_ref.shape[1]
    quarter = channels // GROUP
    blocks = tokens // SUB
    homes = [(ref, n) for ref in x_refs for n in range(ref.shape[1] // 128)]
    tiles = len(homes)
    rings = [(feat_ref, feat_ring), (write_ref, write_ring), (read_ref, read_ring)]
    sources = [(feat_ring, n) for n in range(tiles)] + [(write_ring, 0), (read_ring, 0)]

    def copies(b):
        slot = lax.rem(b, RING)
        at = pl.ds(pl.multiple_of(b * SUB, SUB), SUB)
        return [
            pltpu.make_async_copy(ref.at[at, :], ring.at[slot], sems.at[n, slot])
            for n, (ref, ring) in enumerate(rings)
        ]

    for b in range(RING):
        for copy in copies(jnp.int32(b)):
            copy.start()
    halo = halo_ref[...].astype(F32)[8:16] * place_ref[1].astype(F32)
    for n, buf in enumerate(bufs):
        buf[SUB : SUB + 8, :] = halo[:, n * 128 : (n + 1) * 128]
    carry[...] = jnp.zeros_like(carry)
    zero = place_ref[2]

    def block(b, _):
        here = pl.ds(pl.multiple_of(b * SUB, SUB), SUB)
        slot = lax.rem(b, RING)
        table = table_ref[here, :]
        for copy in copies(b):
            copy.wait()

        def conv(n, taps, tile):
            buf = bufs[n]
            source, spot = sources[n]
            buf[0:8, :] = buf[SUB : SUB + 8, :]
            buf[8:, :] = source[slot, :, pl.ds(spot * 128, 128)].astype(F32)
            return conv_silu(buf, zero, SUB, 0.5 * taps[:, pl.ds(tile * 128, 128)])

        wt = conv(tiles, state_taps_ref, 0).T.astype(BF16)
        wt_ref[:, here] = wt
        c_ref[here, :] = conv(tiles + 1, state_taps_ref, 1).astype(BF16)
        decayed = []
        for n, (x_ref, spot) in enumerate(homes):
            x = conv(n, taps_ref, n)
            x_ref[here, pl.ds(spot * 128, 128)] = x
            decayed.append((x * per_head(table, 2, heads, head_dim, n)).astype(BF16))
            if len(decayed) == WIDE // 128:
                q, off = divmod((n + 1) * 128 - WIDE, quarter)
                carry[q, :, pl.ds(off, WIDE)] += dot(wt, jnp.concatenate(decayed, axis=1))
                decayed = []

        @pl.when(b + RING < blocks)
        def _():
            for copy in copies(b + RING):
                copy.start()

        return 0

    lax.fori_loop(0, blocks, block, 0)
    place = place_ref[0]
    for q in range(GROUP):
        slot = lax.bitwise_xor(place, q)
        msg_ref[slot, 0:state, :] = carry[q].astype(BF16)
        decay = jnp.broadcast_to(rows_ref[blocks : blocks + 1, q * quarter : (q + 1) * quarter], (16, quarter))
        msg_ref[slot, state:, :] = split_pair(decay, iota((16, quarter), 0) == 1)


def conv_states(parts, place, halo, features, state_write, state_read, conv_feat, conv_state, table, rows, heads):
    tokens, channels = features.shape
    state = state_write.shape[1]
    quarter = channels // GROUP
    count = (channels + 2 * state) // 128
    return pl.pallas_call(
        functools.partial(conv_kernel, heads, count),
        in_specs=[SMEM, VMEM] + [ANY] * 3 + [VMEM] * 4,
        out_specs=[VMEM] * (len(parts) + 3),
        out_shape=[pltpu.VMEM((tokens, part), F32) for part in parts]
        + [
            pltpu.VMEM((state, tokens), BF16),
            pltpu.VMEM((tokens, state), BF16),
            jax.ShapeDtypeStruct((GROUP, state + 16, quarter), BF16),
        ],
        scratch_shapes=[
            pltpu.VMEM((GROUP, state, quarter), F32),
            pltpu.VMEM((RING, SUB, channels), BF16),
            pltpu.VMEM((RING, SUB, state), BF16),
            pltpu.VMEM((RING, SUB, state), BF16),
            pltpu.SemaphoreType.DMA((3, RING)),
        ]
        + [pltpu.VMEM((SUB + 8, 128), F32)] * count,
        compiler_params=pltpu.CompilerParams(vmem_limit_bytes=8 * MIB),
        cost_estimate=pl.CostEstimate(flops=10**10, bytes_accessed=10**7, transcendentals=10**6),
        name="conv_states",
    )(place, halo, *map(in_hbm, (features, state_write, state_read)), conv_feat, conv_state, table, rows)


def scores_kernel(c_ref, wt_ref, sc_ref):
    state = c_ref.shape[1]
    keep = iota((SUB, SUB), 0) >= iota((SUB, SUB), 1)

    for b in range(c_ref.shape[0] // SUB):
        at = pl.ds(b * SUB, SUB)
        c = c_ref[at, :]
        sc_ref[at, 0:SUB] = jnp.where(keep, dot(c, wt_ref[:, at]), 0.0).astype(BF16)
        sc_ref[at, SUB : SUB + state] = c


def block_scores(c, wt):
    tokens, state = c.shape
    return pl.pallas_call(
        scores_kernel,
        in_specs=[VMEM, VMEM],
        out_specs=VMEM,
        out_shape=pltpu.VMEM((tokens, SUB + state), BF16),
        compiler_params=pltpu.CompilerParams(vmem_limit_bytes=8 * MIB),
        cost_estimate=pl.CostEstimate(flops=10**9, bytes_accessed=2 * 10**6, transcendentals=0),
        name="block_scores",
    )(c, wt)


def within_kernel(offset, heads, _, x_ref, sc_ref, wt_ref, table_ref, pair_ref, rows_ref, first_ref, out_ref, start):
    blocks = x_ref.shape[0] // SUB
    head_dim = rows_ref.shape[1] // heads
    start[...] = jnp.zeros_like(start)

    def block(b, _):
        at = pl.ds(pl.multiple_of(b * SUB, SUB), SUB)
        table = table_ref[at, :]
        pair = pair_ref[at, :]
        sc = sc_ref[at, :]
        wt = wt_ref[:, at]
        for n in range(x_ref.shape[1] // WIDE):
            cols = pl.ds(offset + n * WIDE, WIDE)
            here = pl.ds(n * WIDE, WIDE)
            tiles = [(offset + n * WIDE + lane) // 128 for lane in range(0, WIDE, 128)]
            x = x_ref[at, here]
            bx = (x * jnp.concatenate([per_head(table, 1, heads, head_dim, t) for t in tiles], axis=1)).astype(BF16)
            now = start[n]
            inner = dot(sc, jnp.concatenate([bx, now.astype(BF16)], axis=0))
            if n % 2:
                outer = jnp.concatenate([per_head(table, 0, heads, head_dim, t) for t in tiles], axis=1)
            else:
                outer = dot(pair, first_ref[:, cols])
            out_ref[at, here] = outer * inner + rows_ref[blocks + 1 : blocks + 2, cols] * x
            start[n] = rows_ref[pl.ds(b, 1), cols] * (now + dot(wt, bx))
        return 0

    lax.fori_loop(0, blocks, block, 0, unroll=UNROLL)


def within(offset, heads, after, x, sc, wt, table, pair, rows, first):
    tokens, part = x.shape
    state = wt.shape[0]
    return pl.pallas_call(
        functools.partial(within_kernel, offset, heads),
        in_specs=[ANY] + [VMEM] * 7,
        out_specs=VMEM,
        out_shape=pltpu.VMEM((tokens, part), F32),
        scratch_shapes=[pltpu.VMEM((part // WIDE, state, WIDE), F32)],
        compiler_params=pltpu.CompilerParams(vmem_limit_bytes=8 * MIB),
        cost_estimate=pl.CostEstimate(flops=2 * 10**9, bytes_accessed=16 * tokens * part, transcendentals=0),
        name="within",
    )(after, x, sc, wt, table, pair, rows, first)


def group_kernel(place_ref, msg_ref, r1_ref, r2_ref, r3_ref, total_ref, prefix_ref, decay_ref, held):
    place = place_ref[0]
    state = prefix_ref.shape[1]
    held[place] = msg_ref[0]
    for k, ref in enumerate((r1_ref, r2_ref, r3_ref)):
        held[lax.bitwise_xor(place, k + 1)] = ref[...]
    sofar = jnp.zeros(prefix_ref.shape[1:], F32)
    decays = jnp.ones((1, sofar.shape[1]), F32)
    for j in range(GROUP):
        tail = held[j, state:, :].astype(F32)
        decay = tail[0:1] + tail[1:2]
        prefix_ref[j] = sofar
        decay_ref[j : j + 1, :] = decays
        sofar = decay * sofar + held[j, 0:state, :].astype(F32)
        decays = decay * decays
    total_ref[0:state, :] = sofar.astype(BF16)
    wide = jnp.broadcast_to(decays, (16, decays.shape[1]))
    total_ref[state:, :] = split_pair(wide, iota(wide.shape, 0) == 1)


def group_prefix(place, msg, received):
    _, rows, quarter = msg.shape
    state = rows - 16
    return pl.pallas_call(
        group_kernel,
        in_specs=[SMEM] + [VMEM] * 4,
        out_specs=[VMEM] * 3,
        out_shape=[
            jax.ShapeDtypeStruct((rows, quarter), BF16),
            pltpu.VMEM((GROUP, state, quarter), F32),
            pltpu.VMEM((8, quarter), F32),
        ],
        scratch_shapes=[pltpu.VMEM((GROUP, rows, quarter), BF16)],
        compiler_params=pltpu.CompilerParams(vmem_limit_bytes=8 * MIB),
        name="group_prefix",
    )(place, msg, *received)


def spread_kernel(place_ref, prefix_ref, decay_ref, carried_ref, *out_refs):
    place = place_ref[0]
    state = prefix_ref.shape[1]
    carried = carried_ref[0:state, :].astype(F32) * place_ref[3].astype(F32)
    for k, ref in enumerate(out_refs):
        j = lax.bitwise_xor(place, k)
        ref[...] = (prefix_ref[j] + decay_ref[pl.ds(j, 1), :] * carried).astype(BF16)


def spread(place, prefix, decay, carried):
    _, state, quarter = prefix.shape
    return pl.pallas_call(
        spread_kernel,
        in_specs=[SMEM] + [VMEM] * 3,
        out_specs=[VMEM] * GROUP,
        out_shape=[jax.ShapeDtypeStruct((state, quarter), BF16)] * GROUP,
        compiler_params=pltpu.CompilerParams(vmem_limit_bytes=8 * MIB),
        name="spread",
    )(place, prefix, decay, carried)


def state_kernel(count, heads, place_ref, c_ref, table_ref, pair_ref, second_ref, s0, s1, s2, s3, *refs):
    m_refs, out_refs, (sq_ref, start) = refs[:count], refs[count : 2 * count], refs[2 * count :]
    place = place_ref[0]
    tokens = c_ref.shape[0]
    quarter = s0.shape[1]
    head_dim = quarter * GROUP // heads
    for k, ref in enumerate((s0, s1, s2, s3)):
        start[lax.bitwise_xor(place, k)] = ref[...]
    homes = [(m, o, n) for m, o in zip(m_refs, out_refs) for n in range(m.shape[1] // WIDE)]

    def block(b, _):
        at = pl.ds(pl.multiple_of(b * SUB, SUB), SUB)
        c = c_ref[at, :]
        table = table_ref[at, :]
        pair = pair_ref[at, :]
        squares = jnp.zeros((SUB, 128), F32)
        for chunk, (m_ref, out_ref, n) in enumerate(homes):
            q, off = divmod(chunk * WIDE, quarter)
            inner = dot(c, start[q, :, off : off + WIDE])
            if chunk % 8 in (0, 3, 6):
                factors = dot(pair, second_ref[:, pl.ds(chunk * WIDE, WIDE)])
            for lane in range(0, WIDE, 128):
                spot = pl.ds(n * WIDE + lane, 128)
                if chunk % 8 in (0, 3, 6):
                    factor = factors[:, lane : lane + 128]
                else:
                    factor = per_head(table, 3, heads, head_dim, (chunk * WIDE + lane) // 128)
                piece = m_ref[at, spot] + factor * inner[:, lane : lane + 128]
                out_ref[at, spot] = piece.astype(BF16)
                squares = squares + piece * piece
        sq_ref[pl.ds(b, 1), :] = jnp.sum(squares.T, axis=0, keepdims=True)
        return 0

    lax.fori_loop(0, tokens // SUB, block, 0, unroll=2)


def add_states(heads, place, ms, c, table, pair, second, pieces):
    tokens, state = c.shape
    quarter = pieces[0].shape[1]
    blocks = tokens // SUB
    return pl.pallas_call(
        functools.partial(state_kernel, len(ms), heads),
        in_specs=[SMEM] + [VMEM] * (4 + GROUP + len(ms)),
        out_specs=[VMEM] * (len(ms) + 1),
        out_shape=[pltpu.VMEM(m.shape, BF16) for m in ms] + [jax.ShapeDtypeStruct((blocks, SUB), F32)],
        scratch_shapes=[pltpu.VMEM((GROUP, state, quarter), BF16)],
        compiler_params=pltpu.CompilerParams(vmem_limit_bytes=8 * MIB),
        name="add_states",
    )(place, c, table, pair, second, *pieces, *ms)


def norm_kernel(size, count, gain_ref, *refs):
    m_refs, sq_refs, (out_ref, ring, sems) = refs[:count], refs[count:-3], refs[-3:]
    homes = [(m, n) for m in m_refs for n in range(m.shape[1] // 128)]
    blocks = out_ref.shape[0] // ROWS

    def copy(b):
        slot = lax.rem(b, RING)
        at = pl.ds(pl.multiple_of(b * ROWS, ROWS), ROWS)
        return pltpu.make_async_copy(ring.at[slot], out_ref.at[at, :], sems.at[slot])

    def block(b, _):
        slot = lax.rem(b, RING)

        @pl.when(b >= RING)
        def _():
            copy(b - RING).wait()

        for sub in range(ROWS // SUB):
            row = b * (ROWS // SUB) + sub
            total = sq_refs[0][pl.ds(row, 1), :]
            for ref in sq_refs[1:]:
                total = total + ref[pl.ds(row, 1), :]
            scale = lax.rsqrt(total * (1.0 / size) + EPSILON)
            scale = jnp.broadcast_to(scale, (SUB, SUB)).T
            at = pl.ds(pl.multiple_of(row * SUB, SUB), SUB)
            for tile, (m_ref, n) in enumerate(homes):
                cols = pl.ds(tile * 128, 128)
                value = m_ref[at, pl.ds(n * 128, 128)].astype(F32) * scale * gain_ref[:, cols]
                ring[slot, pl.ds(sub * SUB, SUB), cols] = value.astype(BF16)
        copy(b).start()
        return 0

    lax.fori_loop(0, blocks, block, 0)
    for b in range(max(0, blocks - RING), blocks):
        copy(jnp.int32(b)).wait()


def norm(size, ms, gain, squares):
    tokens = ms[0].shape[0]
    channels = gain.shape[0]
    return pl.pallas_call(
        functools.partial(norm_kernel, size, len(ms)),
        in_specs=[VMEM] * (1 + len(ms) + len(squares)),
        out_specs=ANY,
        out_shape=jax.ShapeDtypeStruct((tokens, channels), BF16),
        scratch_shapes=[pltpu.VMEM((RING, ROWS, channels), BF16), pltpu.SemaphoreType.DMA((RING,))],
        compiler_params=pltpu.CompilerParams(vmem_limit_bytes=8 * MIB),
        name="norm",
    )(gain.reshape(1, channels), *ms, *squares)


def later(value, steps):
    count = lax.axis_size("seq")
    return lax.ppermute(value, "seq", [(i, (i + steps) % count) for i in range(count)])


def partner(value, axis, mask):
    return lax.ppermute(value, axis, [(i, i ^ mask) for i in range(lax.axis_size(axis))])


def group_carry(total):
    groups = lax.axis_size("seq") // GROUP
    group = lax.axis_index("seq") // GROUP
    carried = later(total, GROUP)
    state = total.shape[0] - 16
    reach = 1
    while reach < groups - 1:
        mine = jnp.where(group >= 1, carried.astype(F32), 0.0)
        got = jnp.where(group >= reach, later(mine.astype(BF16), reach * GROUP).astype(F32), 0.0)
        decay = mine[state : state + 1] + mine[state + 1 : state + 2]
        got_decay = got[state : state + 1] + got[state + 1 : state + 2]
        values = mine[:state] + decay * got[:state]
        both = decay * got_decay
        high = both.astype(BF16)
        rest = (both - high.astype(F32)).astype(BF16)
        carried = jnp.concatenate(
            [values.astype(BF16), high, rest, jnp.zeros((14, both.shape[1]), BF16)], axis=0
        )
        reach *= 2
    return carried


def on_device(
    features, state_write, state_read, conv_feat, conv_state, log_decay, skip_weight, norm_gain
):
    tokens, channels = features.shape
    heads = log_decay.shape[1]
    index = lax.axis_index("seq").astype(jnp.int32)
    place = jnp.stack(
        [lax.rem(index, GROUP), jnp.minimum(index, 1), jnp.zeros_like(index), jnp.minimum(index // GROUP, 1)]
    )
    halo = later(tail_rows(features, state_write, state_read), 1)
    table, pair, rows, first, second = decay_prep(log_decay, skip_weight, channels)
    chunks = channels // WIDE
    cuts = [0, (3 * chunks) // 8 * WIDE, (5 * chunks) // 8 * WIDE, channels]
    parts = [cuts[n + 1] - cuts[n] for n in range(3)]
    *xs, wt, c, msg = conv_states(
        parts, place, halo, features, state_write, state_read, conv_feat, conv_state, table, rows, heads
    )
    received = [partner(msg[k], "seq", k) for k in range(1, GROUP)]
    sc = block_scores(c, wt)
    shared = (sc, wt, table, pair, rows, first)
    ms = [within(cuts[0], heads, place, xs[0], *shared)]
    total, prefix, decay = group_prefix(place, msg, received)
    carried = group_carry(total)
    ms.append(within(cuts[1], heads, total, xs[1], *shared))
    pieces = spread(place, prefix, decay, carried)
    starts = [pieces[0]] + [partner(pieces[k], "seq", k) for k in range(1, GROUP)]
    ms.append(within(cuts[2], heads, pieces[0], xs[2], *shared))
    *ms, squares = add_states(heads, place, ms, c, table, pair, second, starts)
    others = [partner(squares, "head", k) for k in range(1, lax.axis_size("head"))]
    size = channels * lax.axis_size("head")
    return norm(size, ms, norm_gain, [squares] + others)


def solution(mesh):
    placed = (
        P("seq", "head"),
        P("seq", None),
        P("seq", None),
        P(None, "head"),
        P(),
        P("seq", "head"),
        P("head"),
        P("head"),
    )
    return jax.shard_map(
        on_device, mesh=mesh, in_specs=placed, out_specs=P("seq", "head"), check_vma=False
    )
```

```python
import functools

import jax
import jax.numpy as jnp
from jax import lax
from jax.experimental import pallas as pl
from jax.experimental.pallas import tpu as pltpu
from jax.sharding import PartitionSpec as P

EPSILON = 1e-05
SPREAD = 16
SUB = 128
WIDE = 256
ROWS = 256
RING = 4
GROUP = 4
UNROLL = 4
F32 = jnp.float32
BF16 = jnp.bfloat16
HIGHEST = lax.Precision.HIGHEST
MIB = 1 << 20

VMEM = pl.BlockSpec(memory_space=pltpu.VMEM)
SMEM = pl.BlockSpec(memory_space=pltpu.SMEM)
ANY = pl.BlockSpec(memory_space=pl.ANY)


def dot(a, b):
    return jnp.dot(a, b, preferred_element_type=F32)


def exact_dot(a, b):
    return jnp.dot(a, b, preferred_element_type=F32, precision=HIGHEST)


def iota(shape, dim):
    return lax.broadcasted_iota(jnp.int32, shape, dim)


def token_of(row):
    return lax.shift_left(row & 7, SPREAD.bit_length() - 1) | lax.shift_right_logical(row, 3)


def row_of(token):
    return 8 * (token % SPREAD) + token // SPREAD


def ordering():
    shape = (SUB, SUB)
    return token_of(iota(shape, 0)) == iota(shape, 1)


def split_pair(value, low):
    high = value.astype(BF16).astype(F32)
    return jnp.where(low, value - high, high).astype(BF16)


def per_head(table, group, heads, head_dim, tile):
    shift = head_dim.bit_length() - 1
    lane = lax.shift_right_logical(iota(table.shape, 1), shift)
    return jnp.take_along_axis(table, lane + (group * heads + tile * (128 // head_dim)), axis=1)


def decay_kernel(heads, ld_ref, skip_ref, table_ref, pair_ref, rows_ref, first_ref, second_ref, cum_ref, sc_ref):
    tokens = ld_ref.shape[0]
    channels = rows_ref.shape[1]
    blocks = tokens // SUB
    dim_shift = (channels // heads).bit_length() - 1
    copies = 128 // heads
    lower = (token_of(iota((SUB, SUB), 0)) >= iota((SUB, SUB), 1)).astype(F32)
    both = jnp.concatenate([ordering().astype(F32), lower], axis=0)
    lane = iota((SUB, 128), 1)
    totals, refs = [], []
    for b in range(blocks):
        at = pl.ds(b * SUB, SUB)
        sums = jnp.concatenate([exact_dot(both, ld_ref[at, :])] * copies, axis=1)
        decay, cumul = sums[:SUB], sums[SUB:]
        y = 2.0 * decay
        series = -y * (1.0 + y * (1 / 2) * (1.0 + y * (1 / 3) * (1.0 + y * (1 / 4) * (1.0 + y * (1 / 5)))))
        cum_ref[at, :] = cumul
        sc_ref[at, :] = jnp.sqrt(jnp.where(y > -0.1, series, 1.0 - jnp.exp(y)))
        totals.append(cumul[SUB - 1 : SUB])
        middle = row_of(SUB // 2 - 1)
        refs.append(cumul[middle : middle + 1])
    zero = jnp.zeros_like(totals[0])
    before = [zero]
    for b in range(blocks - 1):
        before.append(before[-1] + totals[b])
    after = [zero] * blocks
    for b in range(blocks - 2, -1, -1):
        after[b] = after[b + 1] + totals[b + 1]
    row_lane = iota((1, 128), 1)
    negative = (row_lane >= heads) & (row_lane < 3 * heads)
    scaled = (lane >= heads) & (lane < 3 * heads)
    low = (lane & heads) != 0
    for b in range(blocks):
        at = pl.ds(b * SUB, SUB)
        cumul = cum_ref[at, :]
        base = jnp.where(
            row_lane < heads,
            -refs[b],
            jnp.where(row_lane < 2 * heads, refs[b], jnp.where(row_lane < 3 * heads, totals[b], before[b])),
        )
        power = base + jnp.where(negative, -cumul, cumul) + jnp.where(negative & (row_lane >= 2 * heads), after[b], 0.0)
        table_ref[at, :] = jnp.exp(power) * jnp.where(scaled, sc_ref[at, :], 1.0)
        value = jnp.exp(cumul + jnp.where(row_lane < 2 * heads, -refs[b], before[b]))
        pair_ref[at, :] = split_pair(value, low)
    rows = [jnp.exp(totals[b] - refs[b] + refs[b + 1]) for b in range(blocks - 1)] + [zero]
    rows.append(jnp.exp(before[-1] + totals[-1]))
    rows.append(jnp.concatenate([skip_ref[...]] * copies, axis=1))
    rows += [zero] * (rows_ref.shape[0] - len(rows))
    head_of = lax.shift_right_logical(iota((128, channels), 1), dim_shift)
    row = iota((128, channels), 0)
    rows_ref[...] = exact_dot(jnp.concatenate(rows, axis=0), (row == head_of).astype(F32))
    match = (row & (heads - 1)) == head_of
    first_ref[...] = (match & (row < 2 * heads)).astype(F32).astype(BF16)
    second_ref[...] = (match & (row >= 2 * heads) & (row < 4 * heads)).astype(F32).astype(BF16)


def decay_prep(log_decay, skip_weight, channels):
    tokens, heads = log_decay.shape
    blocks = tokens // SUB
    rows = -(-(blocks + 2) // 8) * 8
    return pl.pallas_call(
        functools.partial(decay_kernel, heads),
        in_specs=[VMEM, VMEM],
        out_specs=[VMEM] * 5,
        out_shape=[
            pltpu.VMEM((tokens, 128), F32),
            pltpu.VMEM((tokens, 128), BF16),
            pltpu.VMEM((rows, channels), F32),
            pltpu.VMEM((128, channels), BF16),
            pltpu.VMEM((128, channels), BF16),
        ],
        scratch_shapes=[pltpu.VMEM((tokens, 128), F32), pltpu.VMEM((tokens, 128), F32)],
        compiler_params=pltpu.CompilerParams(vmem_limit_bytes=8 * MIB),
        cost_estimate=pl.CostEstimate(flops=10**9, bytes_accessed=5 * 10**6, transcendentals=10**6),
        name="decay_prep",
    )(log_decay, skip_weight.reshape(1, heads))


def tail_kernel(feat_ref, write_ref, read_ref, out_ref):
    channels = feat_ref.shape[1]
    state = write_ref.shape[1]
    out_ref[:, :channels] = feat_ref[...]
    out_ref[:, channels : channels + state] = write_ref[...]
    out_ref[:, channels + state :] = read_ref[...]


def tail_rows(features, state_write, state_read):
    tokens, channels = features.shape
    state = state_write.shape[1]
    last = tokens // 16 - 1
    return pl.pallas_call(
        tail_kernel,
        grid=(1,),
        in_specs=[pl.BlockSpec((16, width), lambda i: (last, 0)) for width in (channels, state, state)],
        out_specs=pl.BlockSpec((16, channels + 2 * state), lambda i: (0, 0)),
        out_shape=jax.ShapeDtypeStruct((16, channels + 2 * state), BF16),
        compiler_params=pltpu.CompilerParams(vmem_limit_bytes=2 * MIB),
        name="tail_rows",
    )(*map(in_hbm, (features, state_write, state_read)))


def in_hbm(value):
    return pltpu.with_memory_space_constraint(value, pltpu.HBM)


def conv_silu(now, buf, top, taps):
    size = now.shape[0]
    for k in range(3):
        last = pltpu.roll(now[size - 24 + 8 * k : size - 16 + 8 * k], 1, 0)
        edge = pl.ds(8 * k, 8)
        before = buf[size + 24 + 8 * k : size + 32 + 8 * k, :]
        buf[edge, :] = jnp.where(top, before, last)
        buf[size + 24 + 8 * k : size + 32 + 8 * k, :] = last
    buf[24 : size + 24, :] = now
    total = now * taps[3:4]
    for k in (1, 2, 3):
        total = total + buf[24 - 8 * k : size + 24 - 8 * k, :] * taps[3 - k : 4 - k]
    return total + total * jnp.tanh(total)


def conv_kernel(
    heads, count, place_ref, halo_ref, feat_ref, write_ref, read_ref, taps_ref, state_taps_ref, table_ref, rows_ref,
    *refs,
):
    parts = taps_ref.shape[1] // WIDE
    held, bufs = refs[-parts:], refs[-parts - count : -parts]
    *x_refs, wt_ref, c_ref, msg_ref, carry, wt_held, feat_ring, write_ring, read_ring, sems = refs[: -parts - count]
    tokens, channels = feat_ref.shape
    head_dim = channels // heads
    state = write_ref.shape[1]
    quarter = channels // GROUP
    blocks = tokens // SUB
    homes = [(ref, n) for ref in x_refs for n in range(ref.shape[1] // 128)]
    tiles = len(homes)
    rings = [(feat_ref, feat_ring), (write_ref, write_ring), (read_ref, read_ring)]

    def copies(b, source=0):
        slot = lax.rem(b, RING)
        at = pl.ds(pl.multiple_of(source * SUB, SUB), SUB)
        return [
            pltpu.make_async_copy(ref.at[at, :], ring.at[slot], sems.at[n, slot])
            for n, (ref, ring) in enumerate(rings)
        ]

    def start(b, source):
        for copy in copies(b, source):
            copy.start()

    for b in range(RING):
        start(jnp.int32(b), b)
    halo = halo_ref[...].astype(F32) * place_ref[1].astype(F32)
    for n, buf in enumerate(bufs):
        for k in range(3):
            at = pl.ds(SUB + 24 + 8 * k, 8)
            buf[at, :] = jnp.broadcast_to(halo[13 + k : 14 + k, n * 128 : (n + 1) * 128], (8, 128))
    carry[...] = jnp.zeros_like(carry)
    order = ordering().astype(F32).astype(BF16)
    eye = (iota((SUB, SUB), 0) == iota((SUB, SUB), 1)).astype(F32).astype(BF16)
    top = iota((8, 128), 0) == 0

    for ref in (wt_held, *held):
        ref[...] = jnp.zeros_like(ref)

    def add_part(part, wt):
        q, off = divmod(part * WIDE, quarter)
        carry[q, :, pl.ds(off, WIDE)] += dot(wt, held[part][...])

    def block(b, half, wt_before):
        here = pl.ds(pl.multiple_of(b * SUB, SUB), SUB)
        inside = pl.ds(half * SUB, SUB)
        slot = lax.rem(b, RING)
        table = table_ref[here, :]

        def conv(now, n, taps, tile):
            return conv_silu(now, bufs[n], top, 0.5 * taps[:, pl.ds(tile * 128, 128)])

        def states():
            written = conv(dot(order, write_ring[slot]), tiles, state_taps_ref, 0).astype(BF16)
            contract = (((1,), (1,)), ((), ()))
            wt = lax.dot_general(eye, written, contract, preferred_element_type=F32).astype(BF16)
            wt_ref[:, here] = wt
            wt_held[:, inside] = wt
            c_ref[here, :] = conv(dot(order, read_ring[slot]), tiles + 1, state_taps_ref, 1).astype(BF16)

        for n, (x_ref, spot) in enumerate(homes):
            part, lane = divmod(n * 128, WIDE)
            if lane == 0:
                wide = dot(order, feat_ring[slot, :, pl.ds(part * WIDE, WIDE)])
                if half == 0:
                    add_part(part, wt_before)
                if part == parts // 2:
                    states()
            x = conv(wide[:, lane : lane + 128], n, taps_ref, n)
            x_ref[here, pl.ds(spot * 128, 128)] = x
            held[part][inside, pl.ds(lane, 128)] = (x * per_head(table, 2, heads, head_dim, n)).astype(BF16)

    def pair(i, _):
        first = 2 * i
        for b in (first, first + 1):
            for copy in copies(b):
                copy.wait()
        wt_before = wt_held[...]
        block(first, 0, wt_before)
        block(first + 1, 1, None)
        for b in (first, first + 1):
            start(b, jnp.minimum(b + RING, blocks - 1))
        return 0

    lax.fori_loop(0, blocks // 2, pair, 0)
    for b in range(blocks, blocks + RING):
        for copy in copies(jnp.int32(b)):
            copy.wait()
    wt = wt_held[...]
    for part in range(parts):
        add_part(part, wt)
    place = place_ref[0]
    for q in range(GROUP):
        slot = lax.bitwise_xor(place, q)
        msg_ref[slot, 0:state, :] = carry[q].astype(BF16)
        decay = jnp.broadcast_to(rows_ref[blocks : blocks + 1, q * quarter : (q + 1) * quarter], (16, quarter))
        msg_ref[slot, state:, :] = split_pair(decay, iota((16, quarter), 0) == 1)


def conv_states(parts, place, halo, features, state_write, state_read, conv_feat, conv_state, table, rows, heads):
    tokens, channels = features.shape
    state = state_write.shape[1]
    quarter = channels // GROUP
    count = (channels + 2 * state) // 128
    return pl.pallas_call(
        functools.partial(conv_kernel, heads, count),
        in_specs=[SMEM, VMEM] + [ANY] * 3 + [VMEM] * 4,
        out_specs=[VMEM] * (len(parts) + 3),
        out_shape=[pltpu.VMEM((tokens, part), F32) for part in parts]
        + [
            pltpu.VMEM((state, tokens), BF16),
            pltpu.VMEM((tokens, state), BF16),
            jax.ShapeDtypeStruct((GROUP, state + 16, quarter), BF16),
        ],
        scratch_shapes=[
            pltpu.VMEM((GROUP, state, quarter), F32),
            pltpu.VMEM((state, 2 * SUB), BF16),
            pltpu.VMEM((RING, SUB, channels), BF16),
            pltpu.VMEM((RING, SUB, state), BF16),
            pltpu.VMEM((RING, SUB, state), BF16),
            pltpu.SemaphoreType.DMA((3, RING)),
        ]
        + [pltpu.VMEM((SUB + 48, 128), F32)] * count
        + [pltpu.VMEM((2 * SUB, WIDE), BF16)] * (channels // WIDE),
        compiler_params=pltpu.CompilerParams(vmem_limit_bytes=8 * MIB),
        cost_estimate=pl.CostEstimate(flops=10**10, bytes_accessed=10**7, transcendentals=10**6),
        name="conv_states",
    )(place, halo, *map(in_hbm, (features, state_write, state_read)), conv_feat, conv_state, table, rows)


def scores_kernel(c_ref, wt_ref, sc_ref):
    state = c_ref.shape[1]
    keep = token_of(iota((SUB, SUB), 0)) >= token_of(iota((SUB, SUB), 1))

    for b in range(c_ref.shape[0] // SUB):
        at = pl.ds(b * SUB, SUB)
        c = c_ref[at, :]
        sc_ref[at, 0:SUB] = jnp.where(keep, dot(c, wt_ref[:, at]), 0.0).astype(BF16)
        sc_ref[at, SUB : SUB + state] = c


def block_scores(c, wt):
    tokens, state = c.shape
    return pl.pallas_call(
        scores_kernel,
        in_specs=[VMEM, VMEM],
        out_specs=VMEM,
        out_shape=pltpu.VMEM((tokens, SUB + state), BF16),
        compiler_params=pltpu.CompilerParams(vmem_limit_bytes=8 * MIB),
        cost_estimate=pl.CostEstimate(flops=10**9, bytes_accessed=2 * 10**6, transcendentals=0),
        name="block_scores",
    )(c, wt)


def within_kernel(offset, heads, _, x_ref, sc_ref, wt_ref, table_ref, pair_ref, rows_ref, first_ref, out_ref, start):
    blocks = x_ref.shape[0] // SUB
    head_dim = rows_ref.shape[1] // heads
    start[...] = jnp.zeros_like(start)

    def block(b, _):
        at = pl.ds(pl.multiple_of(b * SUB, SUB), SUB)
        table = table_ref[at, :]
        pair = pair_ref[at, :]
        sc = sc_ref[at, :]
        wt = wt_ref[:, at]
        for n in range(x_ref.shape[1] // WIDE):
            cols = pl.ds(offset + n * WIDE, WIDE)
            here = pl.ds(n * WIDE, WIDE)
            tiles = [(offset + n * WIDE + lane) // 128 for lane in range(0, WIDE, 128)]
            x = x_ref[at, here]
            bx = (x * jnp.concatenate([per_head(table, 1, heads, head_dim, t) for t in tiles], axis=1)).astype(BF16)
            now = start[n]
            inner = dot(sc, jnp.concatenate([bx, now.astype(BF16)], axis=0))
            if n % 2:
                outer = jnp.concatenate([per_head(table, 0, heads, head_dim, t) for t in tiles], axis=1)
            else:
                outer = dot(pair, first_ref[:, cols])
            out_ref[at, here] = outer * inner + rows_ref[blocks + 1 : blocks + 2, cols] * x
            start[n] = rows_ref[pl.ds(b, 1), cols] * (now + dot(wt, bx))
        return 0

    lax.fori_loop(0, blocks, block, 0, unroll=UNROLL)


def within(offset, heads, after, x, sc, wt, table, pair, rows, first):
    tokens, part = x.shape
    state = wt.shape[0]
    return pl.pallas_call(
        functools.partial(within_kernel, offset, heads),
        in_specs=[ANY] + [VMEM] * 7,
        out_specs=VMEM,
        out_shape=pltpu.VMEM((tokens, part), F32),
        scratch_shapes=[pltpu.VMEM((part // WIDE, state, WIDE), F32)],
        compiler_params=pltpu.CompilerParams(vmem_limit_bytes=8 * MIB),
        cost_estimate=pl.CostEstimate(flops=2 * 10**9, bytes_accessed=16 * tokens * part, transcendentals=0),
        name="within",
    )(after, x, sc, wt, table, pair, rows, first)


def group_kernel(place_ref, msg_ref, r1_ref, r2_ref, r3_ref, total_ref, prefix_ref, decay_ref, held):
    place = place_ref[0]
    state = prefix_ref.shape[1]
    held[place] = msg_ref[0]
    for k, ref in enumerate((r1_ref, r2_ref, r3_ref)):
        held[lax.bitwise_xor(place, k + 1)] = ref[...]
    sofar = jnp.zeros(prefix_ref.shape[1:], F32)
    decays = jnp.ones((1, sofar.shape[1]), F32)
    for j in range(GROUP):
        tail = held[j, state:, :].astype(F32)
        decay = tail[0:1] + tail[1:2]
        prefix_ref[j] = sofar
        decay_ref[j : j + 1, :] = decays
        sofar = decay * sofar + held[j, 0:state, :].astype(F32)
        decays = decay * decays
    total_ref[0:state, :] = sofar.astype(BF16)
    wide = jnp.broadcast_to(decays, (16, decays.shape[1]))
    total_ref[state:, :] = split_pair(wide, iota(wide.shape, 0) == 1)


def group_prefix(place, msg, received):
    _, rows, quarter = msg.shape
    state = rows - 16
    return pl.pallas_call(
        group_kernel,
        in_specs=[SMEM] + [VMEM] * 4,
        out_specs=[VMEM] * 3,
        out_shape=[
            jax.ShapeDtypeStruct((rows, quarter), BF16),
            pltpu.VMEM((GROUP, state, quarter), F32),
            pltpu.VMEM((8, quarter), F32),
        ],
        scratch_shapes=[pltpu.VMEM((GROUP, rows, quarter), BF16)],
        compiler_params=pltpu.CompilerParams(vmem_limit_bytes=8 * MIB),
        name="group_prefix",
    )(place, msg, *received)


def spread_kernel(place_ref, prefix_ref, decay_ref, carried_ref, *out_refs):
    place = place_ref[0]
    state = prefix_ref.shape[1]
    carried = carried_ref[0:state, :].astype(F32) * place_ref[3].astype(F32)
    for k, ref in enumerate(out_refs):
        j = lax.bitwise_xor(place, k)
        ref[...] = (prefix_ref[j] + decay_ref[pl.ds(j, 1), :] * carried).astype(BF16)


def spread(place, prefix, decay, carried):
    _, state, quarter = prefix.shape
    return pl.pallas_call(
        spread_kernel,
        in_specs=[SMEM] + [VMEM] * 3,
        out_specs=[VMEM] * GROUP,
        out_shape=[jax.ShapeDtypeStruct((state, quarter), BF16)] * GROUP,
        compiler_params=pltpu.CompilerParams(vmem_limit_bytes=8 * MIB),
        name="spread",
    )(place, prefix, decay, carried)


def state_kernel(count, heads, place_ref, c_ref, table_ref, pair_ref, second_ref, s0, s1, s2, s3, *refs):
    m_refs, out_refs, (sq_ref, start) = refs[:count], refs[count : 2 * count], refs[2 * count :]
    place = place_ref[0]
    tokens = c_ref.shape[0]
    quarter = s0.shape[1]
    head_dim = quarter * GROUP // heads
    for k, ref in enumerate((s0, s1, s2, s3)):
        start[lax.bitwise_xor(place, k)] = ref[...]
    homes = [(m, o, n) for m, o in zip(m_refs, out_refs) for n in range(m.shape[1] // WIDE)]

    def block(b, _):
        at = pl.ds(pl.multiple_of(b * SUB, SUB), SUB)
        c = c_ref[at, :]
        table = table_ref[at, :]
        pair = pair_ref[at, :]
        squares = jnp.zeros((SUB, 128), F32)
        for chunk, (m_ref, out_ref, n) in enumerate(homes):
            q, off = divmod(chunk * WIDE, quarter)
            inner = dot(c, start[q, :, off : off + WIDE])
            if chunk % 8 in (0, 3, 6):
                factors = dot(pair, second_ref[:, pl.ds(chunk * WIDE, WIDE)])
            for lane in range(0, WIDE, 128):
                spot = pl.ds(n * WIDE + lane, 128)
                if chunk % 8 in (0, 3, 6):
                    factor = factors[:, lane : lane + 128]
                else:
                    factor = per_head(table, 3, heads, head_dim, (chunk * WIDE + lane) // 128)
                piece = m_ref[at, spot] + factor * inner[:, lane : lane + 128]
                out_ref[at, spot] = piece.astype(BF16)
                squares = squares + piece * piece
        sq_ref[pl.ds(b, 1), :] = jnp.sum(squares.T, axis=0, keepdims=True)
        return 0

    lax.fori_loop(0, tokens // SUB, block, 0, unroll=UNROLL)


def add_states(heads, place, ms, c, table, pair, second, pieces):
    tokens, state = c.shape
    quarter = pieces[0].shape[1]
    blocks = tokens // SUB
    return pl.pallas_call(
        functools.partial(state_kernel, len(ms), heads),
        in_specs=[SMEM] + [VMEM] * (4 + GROUP + len(ms)),
        out_specs=[VMEM] * (len(ms) + 1),
        out_shape=[pltpu.VMEM(m.shape, BF16) for m in ms] + [jax.ShapeDtypeStruct((blocks, SUB), F32)],
        scratch_shapes=[pltpu.VMEM((GROUP, state, quarter), BF16)],
        compiler_params=pltpu.CompilerParams(vmem_limit_bytes=8 * MIB),
        name="add_states",
    )(place, c, table, pair, second, *pieces, *ms)


def norm_kernel(size, count, gain_ref, *refs):
    m_refs, sq_refs, (out_ref, ring, sems, scales) = refs[:count], refs[count:-4], refs[-4:]
    homes = [(m, n) for m in m_refs for n in range(m.shape[1] // WIDE)]
    blocks = out_ref.shape[0] // ROWS
    total = sq_refs[0][...]
    for ref in sq_refs[1:]:
        total = total + ref[...]
    scales[...] = lax.rsqrt(exact_dot(total, ordering().astype(F32)) * (1.0 / size) + EPSILON)
    back_rows = (iota((SUB, SUB), 0) == token_of(iota((SUB, SUB), 1))).astype(F32).astype(BF16)

    def copy(b):
        slot = b % RING
        return pltpu.make_async_copy(ring.at[slot], out_ref.at[pl.ds(b * ROWS, ROWS), :], sems.at[slot])

    for b in range(blocks):
        slot = b % RING
        if b >= RING:
            copy(b - RING).wait()
        for sub in range(ROWS // SUB):
            row = b * (ROWS // SUB) + sub
            scale = jnp.broadcast_to(scales[row : row + 1, :], (SUB, SUB)).T
            at = pl.ds(row * SUB, SUB)
            for chunk, (m_ref, n) in enumerate(homes):
                rows = dot(back_rows, m_ref[at, pl.ds(n * WIDE, WIDE)])
                for lane in range(0, WIDE, 128):
                    cols = pl.ds(chunk * WIDE + lane, 128)
                    value = rows[:, lane : lane + 128] * scale * gain_ref[:, cols]
                    ring[slot, pl.ds(sub * SUB, SUB), cols] = value.astype(BF16)
        copy(b).start()
    for b in range(max(0, blocks - RING), blocks):
        copy(b).wait()


def norm(size, ms, gain, squares):
    tokens = ms[0].shape[0]
    channels = gain.shape[0]
    return pl.pallas_call(
        functools.partial(norm_kernel, size, len(ms)),
        in_specs=[VMEM] * (1 + len(ms) + len(squares)),
        out_specs=ANY,
        out_shape=jax.ShapeDtypeStruct((tokens, channels), BF16),
        scratch_shapes=[
            pltpu.VMEM((RING, ROWS, channels), BF16),
            pltpu.SemaphoreType.DMA((RING,)),
            pltpu.VMEM(squares[0].shape, F32),
        ],
        compiler_params=pltpu.CompilerParams(vmem_limit_bytes=8 * MIB),
        name="norm",
    )(gain.reshape(1, channels), *ms, *squares)


def later(value, steps):
    count = lax.axis_size("seq")
    return lax.ppermute(value, "seq", [(i, (i + steps) % count) for i in range(count)])


def partner(value, axis, mask):
    return lax.ppermute(value, axis, [(i, i ^ mask) for i in range(lax.axis_size(axis))])


def group_carry(total):
    groups = lax.axis_size("seq") // GROUP
    group = lax.axis_index("seq") // GROUP
    carried = later(total, GROUP)
    state = total.shape[0] - 16
    reach = 1
    while reach < groups - 1:
        mine = jnp.where(group >= 1, carried.astype(F32), 0.0)
        got = jnp.where(group >= reach, later(mine.astype(BF16), reach * GROUP).astype(F32), 0.0)
        decay = mine[state : state + 1] + mine[state + 1 : state + 2]
        got_decay = got[state : state + 1] + got[state + 1 : state + 2]
        values = mine[:state] + decay * got[:state]
        both = decay * got_decay
        high = both.astype(BF16)
        rest = (both - high.astype(F32)).astype(BF16)
        carried = jnp.concatenate(
            [values.astype(BF16), high, rest, jnp.zeros((14, both.shape[1]), BF16)], axis=0
        )
        reach *= 2
    return carried


def on_device(
    features, state_write, state_read, conv_feat, conv_state, log_decay, skip_weight, norm_gain
):
    tokens, channels = features.shape
    heads = log_decay.shape[1]
    index = lax.axis_index("seq").astype(jnp.int32)
    place = jnp.stack(
        [lax.rem(index, GROUP), jnp.minimum(index, 1), jnp.zeros_like(index), jnp.minimum(index // GROUP, 1)]
    )
    halo = later(tail_rows(features, state_write, state_read), 1)
    table, pair, rows, first, second = decay_prep(log_decay, skip_weight, channels)
    chunks = channels // WIDE
    cuts = [0, (3 * chunks) // 8 * WIDE, (6 * chunks) // 8 * WIDE, channels]
    parts = [cuts[n + 1] - cuts[n] for n in range(3)]
    *xs, wt, c, msg = conv_states(
        parts, place, halo, features, state_write, state_read, conv_feat, conv_state, table, rows, heads
    )
    received = [partner(msg[k], "seq", k) for k in range(1, GROUP)]
    sc = block_scores(c, wt)
    shared = (sc, wt, table, pair, rows, first)
    ms = [within(cuts[0], heads, place, xs[0], *shared)]
    total, prefix, decay = group_prefix(place, msg, received)
    carried = group_carry(total)
    ms.append(within(cuts[1], heads, total, xs[1], *shared))
    pieces = spread(place, prefix, decay, carried)
    starts = [pieces[0]] + [partner(pieces[k], "seq", k) for k in range(1, GROUP)]
    ms.append(within(cuts[2], heads, pieces[0], xs[2], *shared))
    *ms, squares = add_states(heads, place, ms, c, table, pair, second, starts)
    others = [partner(squares, "head", k) for k in range(1, lax.axis_size("head"))]
    size = channels * lax.axis_size("head")
    return norm(size, ms, norm_gain, [squares] + others)


def solution(mesh):
    placed = (
        P("seq", "head"),
        P("seq", None),
        P("seq", None),
        P(None, "head"),
        P(),
        P("seq", "head"),
        P("head"),
        P("head"),
    )
    return jax.shard_map(
        on_device, mesh=mesh, in_specs=placed, out_specs=P("seq", "head"), check_vma=False
    )
```

```python
import functools

import jax
import jax.numpy as jnp
from jax import lax
from jax.experimental import pallas as pl
from jax.experimental.pallas import tpu as pltpu
from jax.sharding import PartitionSpec as P

EPSILON = 1e-05
SPREAD = 16
SUB = 128
WIDE = 256
ROWS = 512
RING = 4
GROUP = 4
UNROLL = 4
MXU_CHUNKS = (1,3,5,7)
F32 = jnp.float32
BF16 = jnp.bfloat16
HIGHEST = lax.Precision.HIGHEST
MIB = 1 << 20

VMEM = pl.BlockSpec(memory_space=pltpu.VMEM)
SMEM = pl.BlockSpec(memory_space=pltpu.SMEM)
ANY = pl.BlockSpec(memory_space=pl.ANY)


def dot(a, b):
    return jnp.dot(a, b, preferred_element_type=F32)


def exact_dot(a, b):
    return jnp.dot(a, b, preferred_element_type=F32, precision=HIGHEST)


def iota(shape, dim):
    return lax.broadcasted_iota(jnp.int32, shape, dim)


def token_of(row):
    return lax.shift_left(row & 7, SPREAD.bit_length() - 1) | lax.shift_right_logical(row, 3)


def row_of(token):
    return 8 * (token % SPREAD) + token // SPREAD


def ordering():
    shape = (SUB, SUB)
    return token_of(iota(shape, 0)) == iota(shape, 1)


def split_pair(value, low):
    high = value.astype(BF16).astype(F32)
    return jnp.where(low, value - high, high).astype(BF16)


def per_head(table, group, heads, head_dim, tile):
    shift = head_dim.bit_length() - 1
    lane = lax.shift_right_logical(iota(table.shape, 1), shift)
    return jnp.take_along_axis(table, lane + (group * heads + tile * (128 // head_dim)), axis=1)


def decay_kernel(heads, ld_ref, skip_ref, table_ref, pair_ref, rows_ref, first_ref, second_ref, cum_ref, sc_ref):
    tokens = ld_ref.shape[0]
    channels = rows_ref.shape[1]
    blocks = tokens // SUB
    dim_shift = (channels // heads).bit_length() - 1
    copies = 128 // heads
    lower = (token_of(iota((SUB, SUB), 0)) >= iota((SUB, SUB), 1)).astype(F32)
    both = jnp.concatenate([ordering().astype(F32), lower], axis=0)
    lane = iota((SUB, 128), 1)
    totals, refs = [], []
    for b in range(blocks):
        at = pl.ds(b * SUB, SUB)
        sums = jnp.concatenate([exact_dot(both, ld_ref[at, :])] * copies, axis=1)
        decay, cumul = sums[:SUB], sums[SUB:]
        y = 2.0 * decay
        series = -y * (1.0 + y * (1 / 2) * (1.0 + y * (1 / 3) * (1.0 + y * (1 / 4) * (1.0 + y * (1 / 5)))))
        cum_ref[at, :] = cumul
        sc_ref[at, :] = jnp.sqrt(jnp.where(y > -0.1, series, 1.0 - jnp.exp(y)))
        totals.append(cumul[SUB - 1 : SUB])
        middle = row_of(SUB // 2 - 1)
        refs.append(cumul[middle : middle + 1])
    zero = jnp.zeros_like(totals[0])
    before = [zero]
    for b in range(blocks - 1):
        before.append(before[-1] + totals[b])
    after = [zero] * blocks
    for b in range(blocks - 2, -1, -1):
        after[b] = after[b + 1] + totals[b + 1]
    row_lane = iota((1, 128), 1)
    negative = (row_lane >= heads) & (row_lane < 3 * heads)
    scaled = (lane >= heads) & (lane < 3 * heads)
    low = (lane & heads) != 0
    for b in range(blocks):
        at = pl.ds(b * SUB, SUB)
        cumul = cum_ref[at, :]
        base = jnp.where(
            row_lane < heads,
            -refs[b],
            jnp.where(row_lane < 2 * heads, refs[b], jnp.where(row_lane < 3 * heads, totals[b], before[b])),
        )
        power = base + jnp.where(negative, -cumul, cumul) + jnp.where(negative & (row_lane >= 2 * heads), after[b], 0.0)
        table_ref[at, :] = jnp.exp(power) * jnp.where(scaled, sc_ref[at, :], 1.0)
        value = jnp.exp(cumul + jnp.where(row_lane < 2 * heads, -refs[b], before[b]))
        pair_ref[at, :] = split_pair(value, low)
    rows = [jnp.exp(totals[b] - refs[b] + refs[b + 1]) for b in range(blocks - 1)] + [zero]
    rows.append(jnp.exp(before[-1] + totals[-1]))
    rows.append(jnp.concatenate([skip_ref[...]] * copies, axis=1))
    rows += [zero] * (rows_ref.shape[0] - len(rows))
    head_of = lax.shift_right_logical(iota((128, channels), 1), dim_shift)
    row = iota((128, channels), 0)
    rows_ref[...] = exact_dot(jnp.concatenate(rows, axis=0), (row == head_of).astype(F32))
    match = (row & (heads - 1)) == head_of
    first_ref[...] = (match & (row < 2 * heads)).astype(F32).astype(BF16)
    second_ref[...] = (match & (row >= 2 * heads) & (row < 4 * heads)).astype(F32).astype(BF16)


def decay_prep(log_decay, skip_weight, channels):
    tokens, heads = log_decay.shape
    blocks = tokens // SUB
    rows = -(-(blocks + 2) // 8) * 8
    return pl.pallas_call(
        functools.partial(decay_kernel, heads),
        in_specs=[VMEM, VMEM],
        out_specs=[VMEM] * 5,
        out_shape=[
            pltpu.VMEM((tokens, 128), F32),
            pltpu.VMEM((tokens, 128), BF16),
            pltpu.VMEM((rows, channels), F32),
            pltpu.VMEM((128, channels), BF16),
            pltpu.VMEM((128, channels), BF16),
        ],
        scratch_shapes=[pltpu.VMEM((tokens, 128), F32), pltpu.VMEM((tokens, 128), F32)],
        compiler_params=pltpu.CompilerParams(vmem_limit_bytes=8 * MIB),
        cost_estimate=pl.CostEstimate(flops=10**9, bytes_accessed=5 * 10**6, transcendentals=10**6),
        name="decay_prep",
    )(log_decay, skip_weight.reshape(1, heads))


def tail_kernel(feat_ref, write_ref, read_ref, out_ref):
    channels = feat_ref.shape[1]
    state = write_ref.shape[1]
    out_ref[:, :channels] = feat_ref[...]
    out_ref[:, channels : channels + state] = write_ref[...]
    out_ref[:, channels + state :] = read_ref[...]


def tail_rows(features, state_write, state_read):
    tokens, channels = features.shape
    state = state_write.shape[1]
    last = tokens // 16 - 1
    return pl.pallas_call(
        tail_kernel,
        grid=(1,),
        in_specs=[pl.BlockSpec((16, width), lambda i: (last, 0)) for width in (channels, state, state)],
        out_specs=pl.BlockSpec((16, channels + 2 * state), lambda i: (0, 0)),
        out_shape=jax.ShapeDtypeStruct((16, channels + 2 * state), BF16),
        compiler_params=pltpu.CompilerParams(vmem_limit_bytes=2 * MIB),
        name="tail_rows",
    )(*map(in_hbm, (features, state_write, state_read)))


def in_hbm(value):
    return pltpu.with_memory_space_constraint(value, pltpu.HBM)


def conv_silu(now, buf, top, taps):
    size = now.shape[0]
    for k in range(3):
        last = pltpu.roll(now[size - 24 + 8 * k : size - 16 + 8 * k], 1, 0)
        edge = pl.ds(8 * k, 8)
        before = buf[size + 24 + 8 * k : size + 32 + 8 * k, :]
        buf[edge, :] = jnp.where(top, before, last)
        buf[size + 24 + 8 * k : size + 32 + 8 * k, :] = last
    buf[24 : size + 24, :] = now
    total = now * taps[3:4]
    for k in (1, 2, 3):
        total = total + buf[24 - 8 * k : size + 24 - 8 * k, :] * taps[3 - k : 4 - k]
    return total + total * jnp.tanh(total)


def conv_kernel(
    heads, count, place_ref, halo_ref, feat_ref, write_ref, read_ref, taps_ref, state_taps_ref, table_ref, rows_ref,
    *refs,
):
    parts = taps_ref.shape[1] // WIDE
    held, bufs = refs[-parts:], refs[-parts - count : -parts]
    *x_refs, wt_ref, c_ref, msg_ref, carry, wt_held, feat_ring, write_ring, read_ring, sems = refs[: -parts - count]
    tokens, channels = feat_ref.shape
    head_dim = channels // heads
    state = write_ref.shape[1]
    quarter = channels // GROUP
    blocks = tokens // SUB
    homes = [(ref, n) for ref in x_refs for n in range(ref.shape[1] // 128)]
    tiles = len(homes)
    rings = [(feat_ref, feat_ring), (write_ref, write_ring), (read_ref, read_ring)]

    def copies(b, source=0):
        slot = lax.rem(b, RING)
        at = pl.ds(pl.multiple_of(source * SUB, SUB), SUB)
        return [
            pltpu.make_async_copy(ref.at[at, :], ring.at[slot], sems.at[n, slot])
            for n, (ref, ring) in enumerate(rings)
        ]

    def start(b, source):
        for copy in copies(b, source):
            copy.start()

    for b in range(2):
        start(jnp.int32(b), b)
    halo = halo_ref[...].astype(F32) * place_ref[1].astype(F32)
    for n, buf in enumerate(bufs):
        for k in range(3):
            at = pl.ds(SUB + 24 + 8 * k, 8)
            buf[at, :] = jnp.broadcast_to(halo[13 + k : 14 + k, n * 128 : (n + 1) * 128], (8, 128))
    carry[...] = jnp.zeros_like(carry)
    order = ordering().astype(F32).astype(BF16)
    eye = (iota((SUB, SUB), 0) == iota((SUB, SUB), 1)).astype(F32).astype(BF16)
    top = iota((8, 128), 0) == 0

    for ref in (wt_held, *held):
        ref[...] = jnp.zeros_like(ref)

    def add_part(part, wt):
        q, off = divmod(part * WIDE, quarter)
        carry[q, :, pl.ds(off, WIDE)] += dot(wt, held[part][...])

    def block(b, half, wt_before):
        here = pl.ds(pl.multiple_of(b * SUB, SUB), SUB)
        inside = pl.ds(half * SUB, SUB)
        slot = lax.rem(b, RING)
        table = table_ref[here, :]

        def conv(now, n, taps, tile):
            return conv_silu(now, bufs[n], top, 0.5 * taps[:, pl.ds(tile * 128, 128)])

        def states():
            written = conv(dot(order, write_ring[slot]), tiles, state_taps_ref, 0).astype(BF16)
            contract = (((1,), (1,)), ((), ()))
            wt = lax.dot_general(eye, written, contract, preferred_element_type=F32).astype(BF16)
            wt_ref[:, here] = wt
            wt_held[:, inside] = wt
            c_ref[here, :] = conv(dot(order, read_ring[slot]), tiles + 1, state_taps_ref, 1).astype(BF16)

        for n, (x_ref, spot) in enumerate(homes):
            part, lane = divmod(n * 128, WIDE)
            if lane == 0:
                wide = dot(order, feat_ring[slot, :, pl.ds(part * WIDE, WIDE)])
                if half == 0:
                    add_part(part, wt_before)
                if part == parts // 2:
                    states()
            x = conv(wide[:, lane : lane + 128], n, taps_ref, n)
            x_ref[here, pl.ds(spot * 128, 128)] = x
            held[part][inside, pl.ds(lane, 128)] = (x * per_head(table, 2, heads, head_dim, n)).astype(BF16)

    def pair(i, _):
        first = 2 * i
        for b in (first, first + 1):
            for copy in copies(b):
                copy.wait()
        for b in (first + 2, first + 3):
            start(b, jnp.minimum(b, blocks - 1))
        wt_before = wt_held[...]
        block(first, 0, wt_before)
        block(first + 1, 1, None)
        return 0

    lax.fori_loop(0, blocks // 2, pair, 0)
    for b in range(blocks, blocks + 2):
        for copy in copies(jnp.int32(b)):
            copy.wait()
    wt = wt_held[...]
    for part in range(parts):
        add_part(part, wt)
    place = place_ref[0]
    for q in range(GROUP):
        slot = lax.bitwise_xor(place, q)
        msg_ref[slot, 0:state, :] = carry[q].astype(BF16)
        decay = jnp.broadcast_to(rows_ref[blocks : blocks + 1, q * quarter : (q + 1) * quarter], (16, quarter))
        msg_ref[slot, state:, :] = split_pair(decay, iota((16, quarter), 0) == 1)


def conv_states(parts, place, halo, features, state_write, state_read, conv_feat, conv_state, table, rows, heads):
    tokens, channels = features.shape
    state = state_write.shape[1]
    quarter = channels // GROUP
    count = (channels + 2 * state) // 128
    return pl.pallas_call(
        functools.partial(conv_kernel, heads, count),
        in_specs=[SMEM, VMEM] + [ANY] * 3 + [VMEM] * 4,
        out_specs=[VMEM] * (len(parts) + 3),
        out_shape=[pltpu.VMEM((tokens, part), F32) for part in parts]
        + [
            pltpu.VMEM((state, tokens), BF16),
            pltpu.VMEM((tokens, state), BF16),
            jax.ShapeDtypeStruct((GROUP, state + 16, quarter), BF16),
        ],
        scratch_shapes=[
            pltpu.VMEM((GROUP, state, quarter), F32),
            pltpu.VMEM((state, 2 * SUB), BF16),
            pltpu.VMEM((RING, SUB, channels), BF16),
            pltpu.VMEM((RING, SUB, state), BF16),
            pltpu.VMEM((RING, SUB, state), BF16),
            pltpu.SemaphoreType.DMA((3, RING)),
        ]
        + [pltpu.VMEM((SUB + 48, 128), F32)] * count
        + [pltpu.VMEM((2 * SUB, WIDE), BF16)] * (channels // WIDE),
        compiler_params=pltpu.CompilerParams(vmem_limit_bytes=8 * MIB),
        cost_estimate=pl.CostEstimate(flops=10**10, bytes_accessed=10**7, transcendentals=10**6),
        name="conv_states",
    )(place, halo, *map(in_hbm, (features, state_write, state_read)), conv_feat, conv_state, table, rows)


def scores_kernel(c_ref, wt_ref, sc_ref):
    state = c_ref.shape[1]
    keep = token_of(iota((SUB, SUB), 0)) >= token_of(iota((SUB, SUB), 1))

    for b in range(c_ref.shape[0] // SUB):
        at = pl.ds(b * SUB, SUB)
        c = c_ref[at, :]
        sc_ref[at, 0:SUB] = jnp.where(keep, dot(c, wt_ref[:, at]), 0.0).astype(BF16)
        sc_ref[at, SUB : SUB + state] = c


def block_scores(c, wt):
    tokens, state = c.shape
    return pl.pallas_call(
        scores_kernel,
        in_specs=[VMEM, VMEM],
        out_specs=VMEM,
        out_shape=pltpu.VMEM((tokens, SUB + state), BF16),
        compiler_params=pltpu.CompilerParams(vmem_limit_bytes=8 * MIB),
        cost_estimate=pl.CostEstimate(flops=10**9, bytes_accessed=2 * 10**6, transcendentals=0),
        name="block_scores",
    )(c, wt)


def within_kernel(offset, heads, _, x_ref, sc_ref, wt_ref, table_ref, pair_ref, rows_ref, first_ref, out_ref, start):
    blocks = x_ref.shape[0] // SUB
    head_dim = rows_ref.shape[1] // heads
    start[...] = jnp.zeros_like(start)

    def block(b, _):
        at = pl.ds(pl.multiple_of(b * SUB, SUB), SUB)
        table = table_ref[at, :]
        pair = pair_ref[at, :]
        sc = sc_ref[at, :]
        wt = wt_ref[:, at]
        for n in range(x_ref.shape[1] // WIDE):
            cols = pl.ds(offset + n * WIDE, WIDE)
            here = pl.ds(n * WIDE, WIDE)
            tiles = [(offset + n * WIDE + lane) // 128 for lane in range(0, WIDE, 128)]
            x = x_ref[at, here]
            bx = (x * jnp.concatenate([per_head(table, 1, heads, head_dim, t) for t in tiles], axis=1)).astype(BF16)
            now = start[n]
            inner = dot(sc, jnp.concatenate([bx, now.astype(BF16)], axis=0))
            if n % 2:
                outer = jnp.concatenate([per_head(table, 0, heads, head_dim, t) for t in tiles], axis=1)
            else:
                outer = dot(pair, first_ref[:, cols])
            out_ref[at, here] = outer * inner + rows_ref[blocks + 1 : blocks + 2, cols] * x
            start[n] = rows_ref[pl.ds(b, 1), cols] * (now + dot(wt, bx))
        return 0

    lax.fori_loop(0, blocks, block, 0, unroll=UNROLL)


def within(offset, heads, after, x, sc, wt, table, pair, rows, first):
    tokens, part = x.shape
    state = wt.shape[0]
    return pl.pallas_call(
        functools.partial(within_kernel, offset, heads),
        in_specs=[ANY] + [VMEM] * 7,
        out_specs=VMEM,
        out_shape=pltpu.VMEM((tokens, part), F32),
        scratch_shapes=[pltpu.VMEM((part // WIDE, state, WIDE), F32)],
        compiler_params=pltpu.CompilerParams(vmem_limit_bytes=8 * MIB),
        cost_estimate=pl.CostEstimate(flops=2 * 10**9, bytes_accessed=16 * tokens * part, transcendentals=0),
        name="within",
    )(after, x, sc, wt, table, pair, rows, first)


def group_kernel(place_ref, msg_ref, r1_ref, r2_ref, r3_ref, total_ref, prefix_ref, decay_ref, held):
    place = place_ref[0]
    state = prefix_ref.shape[1]
    held[place] = msg_ref[0]
    for k, ref in enumerate((r1_ref, r2_ref, r3_ref)):
        held[lax.bitwise_xor(place, k + 1)] = ref[...]
    sofar = jnp.zeros(prefix_ref.shape[1:], F32)
    decays = jnp.ones((1, sofar.shape[1]), F32)
    for j in range(GROUP):
        tail = held[j, state:, :].astype(F32)
        decay = tail[0:1] + tail[1:2]
        prefix_ref[j] = sofar
        decay_ref[j : j + 1, :] = decays
        sofar = decay * sofar + held[j, 0:state, :].astype(F32)
        decays = decay * decays
    total_ref[0:state, :] = sofar.astype(BF16)
    wide = jnp.broadcast_to(decays, (16, decays.shape[1]))
    total_ref[state:, :] = split_pair(wide, iota(wide.shape, 0) == 1)


def group_prefix(place, msg, received):
    _, rows, quarter = msg.shape
    state = rows - 16
    return pl.pallas_call(
        group_kernel,
        in_specs=[SMEM] + [VMEM] * 4,
        out_specs=[VMEM] * 3,
        out_shape=[
            jax.ShapeDtypeStruct((rows, quarter), BF16),
            pltpu.VMEM((GROUP, state, quarter), F32),
            pltpu.VMEM((8, quarter), F32),
        ],
        scratch_shapes=[pltpu.VMEM((GROUP, rows, quarter), BF16)],
        compiler_params=pltpu.CompilerParams(vmem_limit_bytes=8 * MIB),
        name="group_prefix",
    )(place, msg, *received)


def spread_kernel(place_ref, prefix_ref, decay_ref, carried_ref, *out_refs):
    place = place_ref[0]
    state = prefix_ref.shape[1]
    carried = carried_ref[0:state, :].astype(F32) * place_ref[3].astype(F32)
    for k, ref in enumerate(out_refs):
        j = lax.bitwise_xor(place, k)
        ref[...] = (prefix_ref[j] + decay_ref[pl.ds(j, 1), :] * carried).astype(BF16)


def spread(place, prefix, decay, carried):
    _, state, quarter = prefix.shape
    return pl.pallas_call(
        spread_kernel,
        in_specs=[SMEM] + [VMEM] * 3,
        out_specs=[VMEM] * GROUP,
        out_shape=[jax.ShapeDtypeStruct((state, quarter), BF16)] * GROUP,
        compiler_params=pltpu.CompilerParams(vmem_limit_bytes=8 * MIB),
        name="spread",
    )(place, prefix, decay, carried)


def state_kernel(count, heads, place_ref, c_ref, table_ref, pair_ref, second_ref, s0, s1, s2, s3, *refs):
    m_refs, out_refs, (sq_ref, start) = refs[:count], refs[count : 2 * count], refs[2 * count :]
    place = place_ref[0]
    tokens = c_ref.shape[0]
    quarter = s0.shape[1]
    head_dim = quarter * GROUP // heads
    for k, ref in enumerate((s0, s1, s2, s3)):
        start[lax.bitwise_xor(place, k)] = ref[...]
    homes = [(m, o, n) for m, o in zip(m_refs, out_refs) for n in range(m.shape[1] // WIDE)]

    def block(b, _):
        at = pl.ds(pl.multiple_of(b * SUB, SUB), SUB)
        c = c_ref[at, :]
        table = table_ref[at, :]
        pair = pair_ref[at, :]
        squares = jnp.zeros((SUB, 128), F32)
        for chunk, (m_ref, out_ref, n) in enumerate(homes):
            q, off = divmod(chunk * WIDE, quarter)
            inner = dot(c, start[q, :, off : off + WIDE])
            if chunk % 8 in MXU_CHUNKS:
                factors = dot(pair, second_ref[:, pl.ds(chunk * WIDE, WIDE)])
            for lane in range(0, WIDE, 128):
                spot = pl.ds(n * WIDE + lane, 128)
                if chunk % 8 in MXU_CHUNKS:
                    factor = factors[:, lane : lane + 128]
                else:
                    factor = per_head(table, 3, heads, head_dim, (chunk * WIDE + lane) // 128)
                piece = m_ref[at, spot] + factor * inner[:, lane : lane + 128]
                out_ref[at, spot] = piece.astype(BF16)
                squares = squares + piece * piece
        sq_ref[pl.ds(b, 1), :] = jnp.sum(squares.T, axis=0, keepdims=True)
        return 0

    lax.fori_loop(0, tokens // SUB, block, 0, unroll=5)


def add_states(heads, place, ms, c, table, pair, second, pieces):
    tokens, state = c.shape
    quarter = pieces[0].shape[1]
    blocks = tokens // SUB
    return pl.pallas_call(
        functools.partial(state_kernel, len(ms), heads),
        in_specs=[SMEM] + [VMEM] * (4 + GROUP + len(ms)),
        out_specs=[VMEM] * (len(ms) + 1),
        out_shape=[pltpu.VMEM(m.shape, BF16) for m in ms] + [jax.ShapeDtypeStruct((blocks, SUB), F32)],
        scratch_shapes=[pltpu.VMEM((GROUP, state, quarter), BF16)],
        compiler_params=pltpu.CompilerParams(vmem_limit_bytes=8 * MIB),
        name="add_states",
    )(place, c, table, pair, second, *pieces, *ms)


def norm_kernel(size, count, gain_ref, *refs):
    m_refs, sq_refs, (out_ref, ring, sems, scales) = refs[:count], refs[count:-4], refs[-4:]
    homes = [(m, n) for m in m_refs for n in range(m.shape[1] // WIDE)]
    blocks = out_ref.shape[0] // ROWS
    total = sq_refs[0][...]
    for ref in sq_refs[1:]:
        total = total + ref[...]
    scales[...] = lax.rsqrt(exact_dot(total, ordering().astype(F32)) * (1.0 / size) + EPSILON)
    back_rows = (iota((SUB, SUB), 0) == token_of(iota((SUB, SUB), 1))).astype(F32).astype(BF16)

    def copy(b):
        slot = b % RING
        return pltpu.make_async_copy(ring.at[slot], out_ref.at[pl.ds(b * ROWS, ROWS), :], sems.at[slot])

    for b in range(blocks):
        slot = b % RING
        if b >= RING:
            copy(b - RING).wait()
        for sub in range(ROWS // SUB):
            row = b * (ROWS // SUB) + sub
            scale = jnp.broadcast_to(scales[row : row + 1, :], (SUB, SUB)).T
            at = pl.ds(row * SUB, SUB)
            for chunk, (m_ref, n) in enumerate(homes):
                rows = dot(back_rows, m_ref[at, pl.ds(n * WIDE, WIDE)])
                for lane in range(0, WIDE, 128):
                    cols = pl.ds(chunk * WIDE + lane, 128)
                    value = rows[:, lane : lane + 128] * scale * gain_ref[:, cols]
                    ring[slot, pl.ds(sub * SUB, SUB), cols] = value.astype(BF16)
        copy(b).start()
    for b in range(max(0, blocks - RING), blocks):
        copy(b).wait()


def norm(size, ms, gain, squares):
    tokens = ms[0].shape[0]
    channels = gain.shape[0]
    return pl.pallas_call(
        functools.partial(norm_kernel, size, len(ms)),
        in_specs=[VMEM] * (1 + len(ms) + len(squares)),
        out_specs=ANY,
        out_shape=jax.ShapeDtypeStruct((tokens, channels), BF16),
        scratch_shapes=[
            pltpu.VMEM((RING, ROWS, channels), BF16),
            pltpu.SemaphoreType.DMA((RING,)),
            pltpu.VMEM(squares[0].shape, F32),
        ],
        compiler_params=pltpu.CompilerParams(vmem_limit_bytes=12 * MIB),
        name="norm",
    )(gain.reshape(1, channels), *ms, *squares)


def later(value, steps):
    count = lax.axis_size("seq")
    return lax.ppermute(value, "seq", [(i, (i + steps) % count) for i in range(count)])


def partner(value, axis, mask):
    return lax.ppermute(value, axis, [(i, i ^ mask) for i in range(lax.axis_size(axis))])


def group_carry(total):
    groups = lax.axis_size("seq") // GROUP
    group = lax.axis_index("seq") // GROUP
    carried = later(total, GROUP)
    state = total.shape[0] - 16
    reach = 1
    while reach < groups - 1:
        mine = jnp.where(group >= 1, carried.astype(F32), 0.0)
        got = jnp.where(group >= reach, later(mine.astype(BF16), reach * GROUP).astype(F32), 0.0)
        decay = mine[state : state + 1] + mine[state + 1 : state + 2]
        got_decay = got[state : state + 1] + got[state + 1 : state + 2]
        values = mine[:state] + decay * got[:state]
        both = decay * got_decay
        high = both.astype(BF16)
        rest = (both - high.astype(F32)).astype(BF16)
        carried = jnp.concatenate(
            [values.astype(BF16), high, rest, jnp.zeros((14, both.shape[1]), BF16)], axis=0
        )
        reach *= 2
    return carried


def on_device(
    features, state_write, state_read, conv_feat, conv_state, log_decay, skip_weight, norm_gain
):
    tokens, channels = features.shape
    heads = log_decay.shape[1]
    index = lax.axis_index("seq").astype(jnp.int32)
    place = jnp.stack(
        [lax.rem(index, GROUP), jnp.minimum(index, 1), jnp.zeros_like(index), jnp.minimum(index // GROUP, 1)]
    )
    halo = later(tail_rows(features, state_write, state_read), 1)
    table, pair, rows, first, second = decay_prep(log_decay, skip_weight, channels)
    chunks = channels // WIDE
    cuts = [0, (3 * chunks) // 8 * WIDE, (6 * chunks) // 8 * WIDE, channels]
    parts = [cuts[n + 1] - cuts[n] for n in range(3)]
    *xs, wt, c, msg = conv_states(
        parts, place, halo, features, state_write, state_read, conv_feat, conv_state, table, rows, heads
    )
    received = [partner(msg[k], "seq", k) for k in range(1, GROUP)]
    sc = block_scores(c, wt)
    shared = (sc, wt, table, pair, rows, first)
    ms = [within(cuts[0], heads, place, xs[0], *shared)]
    total, prefix, decay = group_prefix(place, msg, received)
    carried = group_carry(total)
    ms.append(within(cuts[1], heads, total, xs[1], *shared))
    pieces = spread(place, prefix, decay, carried)
    starts = [pieces[0]] + [partner(pieces[k], "seq", k) for k in range(1, GROUP)]
    ms.append(within(cuts[2], heads, pieces[0], xs[2], *shared))
    *ms, squares = add_states(heads, place, ms, c, table, pair, second, starts)
    others = [partner(squares, "head", k) for k in range(1, lax.axis_size("head"))]
    size = channels * lax.axis_size("head")
    return norm(size, ms, norm_gain, [squares] + others)


def solution(mesh):
    placed = (
        P("seq", "head"),
        P("seq", None),
        P("seq", None),
        P(None, "head"),
        P(),
        P("seq", "head"),
        P("head"),
        P("head"),
    )
    return jax.shard_map(
        on_device, mesh=mesh, in_specs=placed, out_specs=P("seq", "head"), check_vma=False
    )
```

```python
import functools

import jax
import jax.numpy as jnp
from jax import lax
from jax.experimental import pallas as pl
from jax.experimental.pallas import tpu as pltpu
from jax.sharding import PartitionSpec as P

EPSILON = 1e-05
SPREAD = 16
SUB = 128
WIDE = 256
ROWS = 512
RING = 4
GROUP = 4
UNROLL = 4
TOGETHER = 4
MXU_CHUNKS = (1,3,5,7)
F32 = jnp.float32
BF16 = jnp.bfloat16
HIGHEST = lax.Precision.HIGHEST
MIB = 1 << 20

VMEM = pl.BlockSpec(memory_space=pltpu.VMEM)
SMEM = pl.BlockSpec(memory_space=pltpu.SMEM)
ANY = pl.BlockSpec(memory_space=pl.ANY)


def dot(a, b):
    return jnp.dot(a, b, preferred_element_type=F32)


def exact_dot(a, b):
    return jnp.dot(a, b, preferred_element_type=F32, precision=HIGHEST)


def iota(shape, dim):
    return lax.broadcasted_iota(jnp.int32, shape, dim)


def token_of(row):
    return lax.shift_left(row & 7, SPREAD.bit_length() - 1) | lax.shift_right_logical(row, 3)


def row_of(token):
    return 8 * (token % SPREAD) + token // SPREAD


def ordering():
    shape = (SUB, SUB)
    return token_of(iota(shape, 0)) == iota(shape, 1)


def split_pair(value, low):
    high = value.astype(BF16).astype(F32)
    return jnp.where(low, value - high, high).astype(BF16)


def per_head(table, group, heads, head_dim, tile):
    shift = head_dim.bit_length() - 1
    lane = lax.shift_right_logical(iota(table.shape, 1), shift)
    return jnp.take_along_axis(table, lane + (group * heads + tile * (128 // head_dim)), axis=1)


def decay_kernel(heads, ld_ref, skip_ref, table_ref, pair_ref, rows_ref, first_ref, second_ref, cum_ref, sc_ref):
    tokens = ld_ref.shape[0]
    channels = rows_ref.shape[1]
    blocks = tokens // SUB
    dim_shift = (channels // heads).bit_length() - 1
    copies = 128 // heads
    lower = (token_of(iota((SUB, SUB), 0)) >= iota((SUB, SUB), 1)).astype(F32)
    both = jnp.concatenate([ordering().astype(F32), lower], axis=0)
    lane = iota((SUB, 128), 1)
    totals, refs = [], []
    for b in range(blocks):
        at = pl.ds(b * SUB, SUB)
        sums = jnp.concatenate([exact_dot(both, ld_ref[at, :])] * copies, axis=1)
        decay, cumul = sums[:SUB], sums[SUB:]
        y = 2.0 * decay
        series = -y * (1.0 + y * (1 / 2) * (1.0 + y * (1 / 3) * (1.0 + y * (1 / 4) * (1.0 + y * (1 / 5)))))
        cum_ref[at, :] = cumul
        sc_ref[at, :] = jnp.sqrt(jnp.where(y > -0.1, series, 1.0 - jnp.exp(y)))
        totals.append(cumul[SUB - 1 : SUB])
        middle = row_of(SUB // 2 - 1)
        refs.append(cumul[middle : middle + 1])
    zero = jnp.zeros_like(totals[0])
    before = [zero]
    for b in range(blocks - 1):
        before.append(before[-1] + totals[b])
    after = [zero] * blocks
    for b in range(blocks - 2, -1, -1):
        after[b] = after[b + 1] + totals[b + 1]
    row_lane = iota((1, 128), 1)
    negative = (row_lane >= heads) & (row_lane < 3 * heads)
    scaled = (lane >= heads) & (lane < 3 * heads)
    low = (lane & heads) != 0
    for b in range(blocks):
        at = pl.ds(b * SUB, SUB)
        cumul = cum_ref[at, :]
        base = jnp.where(
            row_lane < heads,
            -refs[b],
            jnp.where(row_lane < 2 * heads, refs[b], jnp.where(row_lane < 3 * heads, totals[b], before[b])),
        )
        power = base + jnp.where(negative, -cumul, cumul) + jnp.where(negative & (row_lane >= 2 * heads), after[b], 0.0)
        table_ref[at, :] = jnp.exp(power) * jnp.where(scaled, sc_ref[at, :], 1.0)
        value = jnp.exp(cumul + jnp.where(row_lane < 2 * heads, -refs[b], before[b]))
        pair_ref[at, :] = split_pair(value, low)
    rows = [jnp.exp(totals[b] - refs[b] + refs[b + 1]) for b in range(blocks - 1)] + [zero]
    rows.append(jnp.exp(before[-1] + totals[-1]))
    rows.append(jnp.concatenate([skip_ref[...]] * copies, axis=1))
    rows += [zero] * (rows_ref.shape[0] - len(rows))
    head_of = lax.shift_right_logical(iota((128, channels), 1), dim_shift)
    row = iota((128, channels), 0)
    rows_ref[...] = exact_dot(jnp.concatenate(rows, axis=0), (row == head_of).astype(F32))
    match = (row & (heads - 1)) == head_of
    first_ref[...] = (match & (row < 2 * heads)).astype(F32).astype(BF16)
    second_ref[...] = (match & (row >= 2 * heads) & (row < 4 * heads)).astype(F32).astype(BF16)


def decay_prep(log_decay, skip_weight, channels):
    tokens, heads = log_decay.shape
    blocks = tokens // SUB
    rows = -(-(blocks + 2) // 8) * 8
    return pl.pallas_call(
        functools.partial(decay_kernel, heads),
        in_specs=[VMEM, VMEM],
        out_specs=[VMEM] * 5,
        out_shape=[
            pltpu.VMEM((tokens, 128), F32),
            pltpu.VMEM((tokens, 128), BF16),
            pltpu.VMEM((rows, channels), F32),
            pltpu.VMEM((128, channels), BF16),
            pltpu.VMEM((128, channels), BF16),
        ],
        scratch_shapes=[pltpu.VMEM((tokens, 128), F32), pltpu.VMEM((tokens, 128), F32)],
        compiler_params=pltpu.CompilerParams(vmem_limit_bytes=8 * MIB),
        cost_estimate=pl.CostEstimate(flops=10**9, bytes_accessed=5 * 10**6, transcendentals=10**6),
        name="decay_prep",
    )(log_decay, skip_weight.reshape(1, heads))


def tail_kernel(feat_ref, write_ref, read_ref, out_ref):
    channels = feat_ref.shape[1]
    state = write_ref.shape[1]
    out_ref[:, :channels] = feat_ref[...]
    out_ref[:, channels : channels + state] = write_ref[...]
    out_ref[:, channels + state :] = read_ref[...]


def tail_rows(features, state_write, state_read):
    tokens, channels = features.shape
    state = state_write.shape[1]
    last = tokens // 16 - 1
    return pl.pallas_call(
        tail_kernel,
        grid=(1,),
        in_specs=[pl.BlockSpec((16, width), lambda i: (last, 0)) for width in (channels, state, state)],
        out_specs=pl.BlockSpec((16, channels + 2 * state), lambda i: (0, 0)),
        out_shape=jax.ShapeDtypeStruct((16, channels + 2 * state), BF16),
        compiler_params=pltpu.CompilerParams(vmem_limit_bytes=2 * MIB),
        name="tail_rows",
    )(*map(in_hbm, (features, state_write, state_read)))


def in_hbm(value):
    return pltpu.with_memory_space_constraint(value, pltpu.HBM)


def conv_silu(now, buf, top, taps):
    size = now.shape[0]
    for k in range(3):
        last = pltpu.roll(now[size - 24 + 8 * k : size - 16 + 8 * k], 1, 0)
        edge = pl.ds(8 * k, 8)
        before = buf[size + 24 + 8 * k : size + 32 + 8 * k, :]
        buf[edge, :] = jnp.where(top, before, last)
        buf[size + 24 + 8 * k : size + 32 + 8 * k, :] = last
    buf[24 : size + 24, :] = now
    total = now * taps[3:4]
    for k in (1, 2, 3):
        total = total + buf[24 - 8 * k : size + 24 - 8 * k, :] * taps[3 - k : 4 - k]
    return total + total * jnp.tanh(total)


def conv_kernel(
    heads, count, place_ref, halo_ref, feat_ref, write_ref, read_ref, taps_ref, state_taps_ref, table_ref, rows_ref,
    *refs,
):
    parts = taps_ref.shape[1] // WIDE
    held, bufs = refs[-parts:], refs[-parts - count : -parts]
    *x_refs, wt_ref, c_ref, msg_ref, carry, wt_held, feat_ring, write_ring, read_ring, sems = refs[: -parts - count]
    tokens, channels = feat_ref.shape
    head_dim = channels // heads
    state = write_ref.shape[1]
    quarter = channels // GROUP
    blocks = tokens // SUB
    homes = [(ref, n) for ref in x_refs for n in range(ref.shape[1] // 128)]
    tiles = len(homes)
    rings = [(feat_ref, feat_ring), (write_ref, write_ring), (read_ref, read_ring)]

    def copies(b, source=0):
        slot = lax.rem(b, 2 * TOGETHER)
        at = pl.ds(pl.multiple_of(source * SUB, SUB), SUB)
        return [
            pltpu.make_async_copy(ref.at[at, :], ring.at[slot], sems.at[n, slot])
            for n, (ref, ring) in enumerate(rings)
        ]

    def start(b, source):
        for copy in copies(b, source):
            copy.start()

    for b in range(TOGETHER):
        start(jnp.int32(b), b)
    halo = halo_ref[...].astype(F32) * place_ref[1].astype(F32)
    for n, buf in enumerate(bufs):
        for k in range(3):
            at = pl.ds(SUB + 24 + 8 * k, 8)
            buf[at, :] = jnp.broadcast_to(halo[13 + k : 14 + k, n * 128 : (n + 1) * 128], (8, 128))
    carry[...] = jnp.zeros_like(carry)
    order = ordering().astype(F32).astype(BF16)
    eye = (iota((SUB, SUB), 0) == iota((SUB, SUB), 1)).astype(F32).astype(BF16)
    top = iota((8, 128), 0) == 0

    for ref in (wt_held, *held):
        ref[...] = jnp.zeros_like(ref)

    def add_part(part, wt):
        q, off = divmod(part * WIDE, quarter)
        carry[q, :, pl.ds(off, WIDE)] += dot(wt, held[part][...])

    def block(b, half, wt_before):
        here = pl.ds(pl.multiple_of(b * SUB, SUB), SUB)
        inside = pl.ds(half * SUB, SUB)
        slot = lax.rem(b, 2 * TOGETHER)
        table = table_ref[here, :]

        def conv(now, n, taps, tile):
            return conv_silu(now, bufs[n], top, 0.5 * taps[:, pl.ds(tile * 128, 128)])

        def states():
            written = conv(dot(order, write_ring[slot]), tiles, state_taps_ref, 0).astype(BF16)
            contract = (((1,), (1,)), ((), ()))
            wt = lax.dot_general(eye, written, contract, preferred_element_type=F32).astype(BF16)
            wt_ref[:, here] = wt
            wt_held[:, inside] = wt
            c_ref[here, :] = conv(dot(order, read_ring[slot]), tiles + 1, state_taps_ref, 1).astype(BF16)

        for n, (x_ref, spot) in enumerate(homes):
            part, lane = divmod(n * 128, WIDE)
            if lane == 0:
                wide = dot(order, feat_ring[slot, :, pl.ds(part * WIDE, WIDE)])
                if half == 0:
                    add_part(part, wt_before)
                if part == parts // 2:
                    states()
            x = conv(wide[:, lane : lane + 128], n, taps_ref, n)
            x_ref[here, pl.ds(spot * 128, 128)] = x.astype(x_ref.dtype)
            held[part][inside, pl.ds(lane, 128)] = (x * per_head(table, 2, heads, head_dim, n)).astype(BF16)

    def step(i, _):
        first = TOGETHER * i
        for k in range(TOGETHER):
            for copy in copies(first + k):
                copy.wait()
        for k in range(TOGETHER, 2 * TOGETHER):
            start(first + k, jnp.minimum(first + k, blocks - 1))
        wt_before = wt_held[...]
        for k in range(TOGETHER):
            block(first + k, k, wt_before)
        return 0

    lax.fori_loop(0, blocks // TOGETHER, step, 0)
    for b in range(blocks, blocks + TOGETHER):
        for copy in copies(jnp.int32(b)):
            copy.wait()
    wt = wt_held[...]
    for part in range(parts):
        add_part(part, wt)
    place = place_ref[0]
    for q in range(GROUP):
        slot = lax.bitwise_xor(place, q)
        msg_ref[slot, 0:state, :] = carry[q].astype(BF16)
        decay = jnp.broadcast_to(rows_ref[blocks : blocks + 1, q * quarter : (q + 1) * quarter], (16, quarter))
        msg_ref[slot, state:, :] = split_pair(decay, iota((16, quarter), 0) == 1)


def conv_states(parts, place, halo, features, state_write, state_read, conv_feat, conv_state, table, rows, heads):
    tokens, channels = features.shape
    state = state_write.shape[1]
    quarter = channels // GROUP
    count = (channels + 2 * state) // 128
    return pl.pallas_call(
        functools.partial(conv_kernel, heads, count),
        in_specs=[SMEM, VMEM] + [ANY] * 3 + [VMEM] * 4,
        out_specs=[VMEM] * (len(parts) + 3),
        out_shape=[pltpu.VMEM((tokens, part), F32 if n == 2 else BF16) for n, part in enumerate(parts)]
        + [
            pltpu.VMEM((state, tokens), BF16),
            pltpu.VMEM((tokens, state), BF16),
            jax.ShapeDtypeStruct((GROUP, state + 16, quarter), BF16),
        ],
        scratch_shapes=[
            pltpu.VMEM((GROUP, state, quarter), F32),
            pltpu.VMEM((state, TOGETHER * SUB), BF16),
            pltpu.VMEM((2 * TOGETHER, SUB, channels), BF16),
            pltpu.VMEM((2 * TOGETHER, SUB, state), BF16),
            pltpu.VMEM((2 * TOGETHER, SUB, state), BF16),
            pltpu.SemaphoreType.DMA((3, 2 * TOGETHER)),
        ]
        + [pltpu.VMEM((SUB + 48, 128), F32)] * count
        + [pltpu.VMEM((TOGETHER * SUB, WIDE), BF16)] * (channels // WIDE),
        compiler_params=pltpu.CompilerParams(vmem_limit_bytes=14 * MIB),
        cost_estimate=pl.CostEstimate(flops=10**10, bytes_accessed=10**7, transcendentals=10**6),
        name="conv_states",
    )(place, halo, *map(in_hbm, (features, state_write, state_read)), conv_feat, conv_state, table, rows)


def scores_kernel(c_ref, wt_ref, sc_ref):
    state = c_ref.shape[1]
    keep = token_of(iota((SUB, SUB), 0)) >= token_of(iota((SUB, SUB), 1))

    for b in range(c_ref.shape[0] // SUB):
        at = pl.ds(b * SUB, SUB)
        c = c_ref[at, :]
        sc_ref[at, 0:SUB] = jnp.where(keep, dot(c, wt_ref[:, at]), 0.0).astype(BF16)
        sc_ref[at, SUB : SUB + state] = c


def block_scores(c, wt):
    tokens, state = c.shape
    return pl.pallas_call(
        scores_kernel,
        in_specs=[VMEM, VMEM],
        out_specs=VMEM,
        out_shape=pltpu.VMEM((tokens, SUB + state), BF16),
        compiler_params=pltpu.CompilerParams(vmem_limit_bytes=8 * MIB),
        cost_estimate=pl.CostEstimate(flops=10**9, bytes_accessed=2 * 10**6, transcendentals=0),
        name="block_scores",
    )(c, wt)


def within_kernel(offset, heads, _, x_ref, sc_ref, wt_ref, table_ref, pair_ref, rows_ref, first_ref, out_ref, start):
    blocks = x_ref.shape[0] // SUB
    head_dim = rows_ref.shape[1] // heads
    start[...] = jnp.zeros_like(start)

    def block(b, _):
        at = pl.ds(pl.multiple_of(b * SUB, SUB), SUB)
        table = table_ref[at, :]
        pair = pair_ref[at, :]
        sc = sc_ref[at, :]
        wt = wt_ref[:, at]
        for n in range(x_ref.shape[1] // WIDE):
            cols = pl.ds(offset + n * WIDE, WIDE)
            here = pl.ds(n * WIDE, WIDE)
            tiles = [(offset + n * WIDE + lane) // 128 for lane in range(0, WIDE, 128)]
            x = x_ref[at, here].astype(F32)
            bx = (x * jnp.concatenate([per_head(table, 1, heads, head_dim, t) for t in tiles], axis=1)).astype(BF16)
            now = start[n]
            inner = dot(sc, jnp.concatenate([bx, now.astype(BF16)], axis=0))
            if n % 2:
                outer = jnp.concatenate([per_head(table, 0, heads, head_dim, t) for t in tiles], axis=1)
            else:
                outer = dot(pair, first_ref[:, cols])
            out_ref[at, here] = outer * inner + rows_ref[blocks + 1 : blocks + 2, cols] * x
            start[n] = rows_ref[pl.ds(b, 1), cols] * (now + dot(wt, bx))
        return 0

    lax.fori_loop(0, blocks, block, 0, unroll=UNROLL)


def within(offset, heads, after, x, sc, wt, table, pair, rows, first):
    tokens, part = x.shape
    state = wt.shape[0]
    return pl.pallas_call(
        functools.partial(within_kernel, offset, heads),
        in_specs=[ANY] + [VMEM] * 7,
        out_specs=VMEM,
        out_shape=pltpu.VMEM((tokens, part), F32),
        scratch_shapes=[pltpu.VMEM((part // WIDE, state, WIDE), F32)],
        compiler_params=pltpu.CompilerParams(vmem_limit_bytes=8 * MIB),
        cost_estimate=pl.CostEstimate(flops=2 * 10**9, bytes_accessed=16 * tokens * part, transcendentals=0),
        name="within",
    )(after, x, sc, wt, table, pair, rows, first)


def group_kernel(place_ref, msg_ref, r1_ref, r2_ref, r3_ref, total_ref, prefix_ref, decay_ref, held):
    place = place_ref[0]
    state = prefix_ref.shape[1]
    held[place] = msg_ref[0]
    for k, ref in enumerate((r1_ref, r2_ref, r3_ref)):
        held[lax.bitwise_xor(place, k + 1)] = ref[...]
    sofar = jnp.zeros(prefix_ref.shape[1:], F32)
    decays = jnp.ones((1, sofar.shape[1]), F32)
    for j in range(GROUP):
        tail = held[j, state:, :].astype(F32)
        decay = tail[0:1] + tail[1:2]
        prefix_ref[j] = sofar
        decay_ref[j : j + 1, :] = decays
        sofar = decay * sofar + held[j, 0:state, :].astype(F32)
        decays = decay * decays
    total_ref[0:state, :] = sofar.astype(BF16)
    wide = jnp.broadcast_to(decays, (16, decays.shape[1]))
    total_ref[state:, :] = split_pair(wide, iota(wide.shape, 0) == 1)


def group_prefix(place, msg, received):
    _, rows, quarter = msg.shape
    state = rows - 16
    return pl.pallas_call(
        group_kernel,
        in_specs=[SMEM] + [VMEM] * 4,
        out_specs=[VMEM] * 3,
        out_shape=[
            jax.ShapeDtypeStruct((rows, quarter), BF16),
            pltpu.VMEM((GROUP, state, quarter), F32),
            pltpu.VMEM((8, quarter), F32),
        ],
        scratch_shapes=[pltpu.VMEM((GROUP, rows, quarter), BF16)],
        compiler_params=pltpu.CompilerParams(vmem_limit_bytes=8 * MIB),
        name="group_prefix",
    )(place, msg, *received)


def spread_kernel(place_ref, prefix_ref, decay_ref, carried_ref, *out_refs):
    place = place_ref[0]
    state = prefix_ref.shape[1]
    carried = carried_ref[0:state, :].astype(F32) * place_ref[3].astype(F32)
    for k, ref in enumerate(out_refs):
        j = lax.bitwise_xor(place, k)
        ref[...] = (prefix_ref[j] + decay_ref[pl.ds(j, 1), :] * carried).astype(BF16)


def spread(place, prefix, decay, carried):
    _, state, quarter = prefix.shape
    return pl.pallas_call(
        spread_kernel,
        in_specs=[SMEM] + [VMEM] * 3,
        out_specs=[VMEM] * GROUP,
        out_shape=[jax.ShapeDtypeStruct((state, quarter), BF16)] * GROUP,
        compiler_params=pltpu.CompilerParams(vmem_limit_bytes=8 * MIB),
        name="spread",
    )(place, prefix, decay, carried)


def state_kernel(count, heads, place_ref, c_ref, table_ref, pair_ref, second_ref, s0, s1, s2, s3, *refs):
    m_refs, out_refs, (sq_ref, start) = refs[:count], refs[count : 2 * count], refs[2 * count :]
    place = place_ref[0]
    tokens = c_ref.shape[0]
    quarter = s0.shape[1]
    head_dim = quarter * GROUP // heads
    for k, ref in enumerate((s0, s1, s2, s3)):
        start[lax.bitwise_xor(place, k)] = ref[...]
    homes = [(m, o, n) for m, o in zip(m_refs, out_refs) for n in range(m.shape[1] // WIDE)]

    def block(b, _):
        at = pl.ds(pl.multiple_of(b * SUB, SUB), SUB)
        c = c_ref[at, :]
        table = table_ref[at, :]
        pair = pair_ref[at, :]
        squares = jnp.zeros((SUB, 128), F32)
        for chunk, (m_ref, out_ref, n) in enumerate(homes):
            q, off = divmod(chunk * WIDE, quarter)
            inner = dot(c, start[q, :, off : off + WIDE])
            if chunk % 8 in MXU_CHUNKS:
                factors = dot(pair, second_ref[:, pl.ds(chunk * WIDE, WIDE)])
            for lane in range(0, WIDE, 128):
                spot = pl.ds(n * WIDE + lane, 128)
                if chunk % 8 in MXU_CHUNKS:
                    factor = factors[:, lane : lane + 128]
                else:
                    factor = per_head(table, 3, heads, head_dim, (chunk * WIDE + lane) // 128)
                piece = m_ref[at, spot] + factor * inner[:, lane : lane + 128]
                out_ref[at, spot] = piece.astype(BF16)
                squares = squares + piece * piece
        sq_ref[pl.ds(b, 1), :] = jnp.sum(squares.T, axis=0, keepdims=True)
        return 0

    lax.fori_loop(0, tokens // SUB, block, 0, unroll=5)


def add_states(heads, place, ms, c, table, pair, second, pieces):
    tokens, state = c.shape
    quarter = pieces[0].shape[1]
    blocks = tokens // SUB
    return pl.pallas_call(
        functools.partial(state_kernel, len(ms), heads),
        in_specs=[SMEM] + [VMEM] * (4 + GROUP + len(ms)),
        out_specs=[VMEM] * (len(ms) + 1),
        out_shape=[pltpu.VMEM(m.shape, BF16) for m in ms] + [jax.ShapeDtypeStruct((blocks, SUB), F32)],
        scratch_shapes=[pltpu.VMEM((GROUP, state, quarter), BF16)],
        compiler_params=pltpu.CompilerParams(vmem_limit_bytes=8 * MIB),
        name="add_states",
    )(place, c, table, pair, second, *pieces, *ms)


def norm_kernel(size, count, gain_ref, *refs):
    m_refs, sq_refs, (out_ref, ring, sems, scales) = refs[:count], refs[count:-4], refs[-4:]
    homes = [(m, n) for m in m_refs for n in range(m.shape[1] // WIDE)]
    blocks = out_ref.shape[0] // ROWS
    total = sq_refs[0][...]
    for ref in sq_refs[1:]:
        total = total + ref[...]
    scales[...] = lax.rsqrt(exact_dot(total, ordering().astype(F32)) * (1.0 / size) + EPSILON)
    back_rows = (iota((SUB, SUB), 0) == token_of(iota((SUB, SUB), 1))).astype(F32).astype(BF16)

    def copy(b):
        slot = b % RING
        return pltpu.make_async_copy(ring.at[slot], out_ref.at[pl.ds(b * ROWS, ROWS), :], sems.at[slot])

    for b in range(blocks):
        slot = b % RING
        if b >= RING:
            copy(b - RING).wait()
        for sub in range(ROWS // SUB):
            row = b * (ROWS // SUB) + sub
            scale = jnp.broadcast_to(scales[row : row + 1, :], (SUB, SUB)).T
            at = pl.ds(row * SUB, SUB)
            for chunk, (m_ref, n) in enumerate(homes):
                rows = dot(back_rows, m_ref[at, pl.ds(n * WIDE, WIDE)])
                for lane in range(0, WIDE, 128):
                    cols = pl.ds(chunk * WIDE + lane, 128)
                    value = rows[:, lane : lane + 128] * scale * gain_ref[:, cols]
                    ring[slot, pl.ds(sub * SUB, SUB), cols] = value.astype(BF16)
        copy(b).start()
    for b in range(max(0, blocks - RING), blocks):
        copy(b).wait()


def norm(size, ms, gain, squares):
    tokens = ms[0].shape[0]
    channels = gain.shape[0]
    return pl.pallas_call(
        functools.partial(norm_kernel, size, len(ms)),
        in_specs=[VMEM] * (1 + len(ms) + len(squares)),
        out_specs=ANY,
        out_shape=jax.ShapeDtypeStruct((tokens, channels), BF16),
        scratch_shapes=[
            pltpu.VMEM((RING, ROWS, channels), BF16),
            pltpu.SemaphoreType.DMA((RING,)),
            pltpu.VMEM(squares[0].shape, F32),
        ],
        compiler_params=pltpu.CompilerParams(vmem_limit_bytes=12 * MIB),
        name="norm",
    )(gain.reshape(1, channels), *ms, *squares)


def later(value, steps):
    count = lax.axis_size("seq")
    return lax.ppermute(value, "seq", [(i, (i + steps) % count) for i in range(count)])


def partner(value, axis, mask):
    return lax.ppermute(value, axis, [(i, i ^ mask) for i in range(lax.axis_size(axis))])


def group_carry(total):
    groups = lax.axis_size("seq") // GROUP
    group = lax.axis_index("seq") // GROUP
    carried = later(total, GROUP)
    state = total.shape[0] - 16
    reach = 1
    while reach < groups - 1:
        mine = jnp.where(group >= 1, carried.astype(F32), 0.0)
        got = jnp.where(group >= reach, later(mine.astype(BF16), reach * GROUP).astype(F32), 0.0)
        decay = mine[state : state + 1] + mine[state + 1 : state + 2]
        got_decay = got[state : state + 1] + got[state + 1 : state + 2]
        values = mine[:state] + decay * got[:state]
        both = decay * got_decay
        high = both.astype(BF16)
        rest = (both - high.astype(F32)).astype(BF16)
        carried = jnp.concatenate(
            [values.astype(BF16), high, rest, jnp.zeros((14, both.shape[1]), BF16)], axis=0
        )
        reach *= 2
    return carried


def on_device(
    features, state_write, state_read, conv_feat, conv_state, log_decay, skip_weight, norm_gain
):
    tokens, channels = features.shape
    heads = log_decay.shape[1]
    index = lax.axis_index("seq").astype(jnp.int32)
    place = jnp.stack(
        [lax.rem(index, GROUP), jnp.minimum(index, 1), jnp.zeros_like(index), jnp.minimum(index // GROUP, 1)]
    )
    halo = later(tail_rows(features, state_write, state_read), 1)
    table, pair, rows, first, second = decay_prep(log_decay, skip_weight, channels)
    chunks = channels // WIDE
    cuts = [0, (3 * chunks) // 8 * WIDE, (6 * chunks) // 8 * WIDE, channels]
    parts = [cuts[n + 1] - cuts[n] for n in range(3)]
    *xs, wt, c, msg = conv_states(
        parts, place, halo, features, state_write, state_read, conv_feat, conv_state, table, rows, heads
    )
    received = [partner(msg[k], "seq", k) for k in range(1, GROUP)]
    sc = block_scores(c, wt)
    shared = (sc, wt, table, pair, rows, first)
    ms = [within(cuts[0], heads, place, xs[0], *shared)]
    total, prefix, decay = group_prefix(place, msg, received)
    carried = group_carry(total)
    ms.append(within(cuts[1], heads, total, xs[1], *shared))
    pieces = spread(place, prefix, decay, carried)
    starts = [pieces[0]] + [partner(pieces[k], "seq", k) for k in range(1, GROUP)]
    ms.append(within(cuts[2], heads, pieces[0], xs[2], *shared))
    *ms, squares = add_states(heads, place, ms, c, table, pair, second, starts)
    others = [partner(squares, "head", k) for k in range(1, lax.axis_size("head"))]
    size = channels * lax.axis_size("head")
    return norm(size, ms, norm_gain, [squares] + others)


def solution(mesh):
    placed = (
        P("seq", "head"),
        P("seq", None),
        P("seq", None),
        P(None, "head"),
        P(),
        P("seq", "head"),
        P("head"),
        P("head"),
    )
    return jax.shard_map(
        on_device, mesh=mesh, in_specs=placed, out_specs=P("seq", "head"), check_vma=False
    )
```
